256 devices in a mesh: dom: 128 (over y, z, x), feat: 2 (over core).
Axes of the slice: x: 4, y: 4, z: 8, core: 2. Of those that a mesh axis runs over, the one named last changes fastest.
Arguments:
- features: bfloat16 [16384, 128], P('dom'), may hold values from -6 to 6
- w_self: bfloat16 [128, 256], P(None, 'feat'), may hold values from -0.5 to 0.5
- w_neigh: bfloat16 [128, 256], P(None, 'feat'), may hold values from -6 to 6
- tiles: bfloat16 [16384, 128, 128], P('dom'), may hold values from 0 to 1, as said below
- dest: int32 [16384, 1], P('dom'), may hold values from 0 to 127; in each aligned block of 128 rows (0 to 127, 128 to 255, ...) at most 2 rows name the same one
- outside: int32 [16384], P('dom'), may hold values from 1 to 256
- cotangent: bfloat16 [16384, 256], P('dom', 'feat'), may hold values from -6 to 6
Outputs:
- output: bfloat16 [16384, 256], P('dom', 'feat')
- grad_input: bfloat16 [16384, 128], P('dom')
- grad_self: float32 [128, 256], P(None, 'feat')
- grad_neigh: float32 [128, 256], P(None, 'feat')
The draws below stay inside these ranges and needn't reach their ends.
Inputs may be any that keep to these rules, and one draw needn't show every extreme that they name: `dest`: among the 128 tiles of one index of dom, at most 2 name one destination block, and some block is named by exactly 2. `tiles`: entries are 0 or 1.
All inputs are finite; a program needn't handle non-finite values.
Results may differ from the reference program's by a relative error of at most 0.015.
Values may be sent and summed in bfloat16 or wider, within the bound.
A program may use at most 128 MiB of HBM per device.

```python
import math
import jax
import jax.numpy as jnp
import numpy as np
from jax import lax

FIN = 128
HID = 256
BLOCK = 128
CAP = 2
TILES_DEV = 128
NODES = 16384
TILES = 16384
N_DOM = 128


def draw_tiles(key, part):
    key = jax.random.fold_in(key, 11)
    links = jax.random.bernoulli(key, 2.0 / BLOCK, (TILES, BLOCK, BLOCK))
    return links.astype(jnp.float32).astype(jnp.bfloat16)


def set_ends(values, own_key, least, largest):
    spot = [jax.random.randint(jax.random.fold_in(own_key, axis), (), 0, length) for axis, length in enumerate(values.shape)]
    widest = values.shape.index(max(values.shape))
    neighbour = spot[:widest] + [(spot[widest] + 1) % values.shape[widest]] + spot[widest + 1:]
    return values.at[tuple(spot)].set(least).at[tuple(neighbour)].set(largest)


def levels(rng, shape, split, smallest, top_value):
    level = 1.0
    for position, parts in split:
        heights = jax.random.uniform(jax.random.fold_in(jax.random.fold_in(rng, 6), position), (parts,), jnp.float32, smallest / len(split), top_value / len(split))
        level = level * jnp.repeat(jnp.exp(heights), shape[position] // parts).reshape((-1,) + (1,) * (len(shape) - 1 - position))
    return level


def shared_out(own_key, own, number, rows, count, top, most, skew):
    order = jax.random.permutation(own_key, count)
    crowded, usual = portions_of(count, rows * top, most, skew, True), portions_of(count, rows * top, most, skew, False)
    places = jnp.arange(count)

    def named(tallies, offset_by):
        used = int((tallies > 0).sum())
        fixed = max(1, used // 4)
        moved = fixed + (places - fixed + offset_by * (used - fixed)) % max(1, count - fixed)
        return jnp.zeros((count,), jnp.int32).at[order[jnp.where(places < fixed, places, moved)]].set(jnp.asarray(tallies, jnp.int32))

    tallies = jnp.where(number % 4 == 0, named(crowded, number // 4), named(usual, number - number // 4 - 1))
    mixed = jax.random.permutation(jax.random.fold_in(own, 3), count)
    source_of, sink = mixed[0:count // 2 * 2:2], mixed[1:count // 2 * 2:2]
    margin = jnp.minimum(tallies[source_of] - 1, most - tallies[sink]) // 2
    margin = jnp.where((source_of == order[0]) | (sink == order[0]) | (tallies[sink] == 0), 0, jnp.maximum(margin, 0))
    moved = jax.random.randint(jax.random.fold_in(own, 4), (count // 2,), 0, 1 << 20) % (margin + 1)
    tallies = tallies.at[source_of].add(-moved).at[sink].add(moved)
    items = jnp.searchsorted(jnp.cumsum(tallies), jnp.arange(rows * top), side="right").astype(jnp.int32)
    table = items.reshape(top, rows).T
    table = table[jax.random.permutation(jax.random.fold_in(own, 1), rows)]
    offset_by = jax.random.randint(jax.random.fold_in(own, 2), (rows, 1), 0, top)
    return jnp.take_along_axis(table, (jnp.arange(top)[None, :] + offset_by) % top, axis=1)


def portions_of(amount, total, bound, lean, full):
    portions = [(1 << 20) // math.isqrt(standing ** lean) + 1 for standing in range(1, amount + 1)]
    largest = bound if full else min(bound, max(-(-total // amount), total * portions[0] // sum(portions)))
    least = 1 if total - largest >= amount - 1 else 0
    given, surplus = [largest] + [least] * (amount - 1), total - largest - least * (amount - 1)
    while surplus > 0:
        candidates = [i for i in range(1, amount) if given[i] < largest] or [i for i in range(1, amount) if given[i] < bound]
        mass, budget = sum([portions[i] for i in candidates]), surplus
        for i in candidates:
            more = min(bound - given[i], max(1, budget * portions[i] // mass), surplus)
            given[i] = given[i] + more
            surplus = surplus - more
    return np.array(given)


def noise(stream_key, extent, width, limit, pieces=(), held_as=jnp.bfloat16):
    result = width * jax.random.normal(stream_key, extent, jnp.float32)
    if pieces:
        result = result * levels(stream_key, extent, pieces, -0.22, 0.18)
    return jnp.clip(result, -limit, limit).astype(held_as)


def setup_inputs(seed: int = 0) -> dict:
    splits = jax.random.split(jax.random.key(seed), 8)
    features = noise(splits[0], (NODES, FIN), 1.0, 6.0, ((0, 128),))
    w_self = noise(splits[1], (FIN, HID), FIN ** -0.5, 0.5, ((1, 2),))
    w_neigh = noise(splits[2], (FIN, HID), 1.0, 6.0, ((1, 2),))
    tiles = draw_tiles(jax.random.fold_in(splits[7], 71), 0)
    dest_keys = jax.random.split(jax.random.fold_in(splits[4], 1), TILES // TILES_DEV)
    dest_turns = jax.random.permutation(jax.random.fold_in(splits[4], 3), TILES // TILES_DEV)
    dest = jax.vmap(lambda own, number: shared_out(jax.random.fold_in(splits[4], 2), own, number, TILES_DEV, N_DOM, 1, CAP, 2))(dest_keys, dest_turns).reshape((TILES, 1))
    outside = set_ends(jax.random.randint(splits[5], (NODES,), 1, 257), jax.random.fold_in(splits[5], 1), 1, 256).astype(jnp.int32)
    cotangent = noise(splits[6], (NODES, HID), 1.0, 6.0, ((0, 128), (1, 2)))
    return {"features": features, "w_self": w_self, "w_neigh": w_neigh, "tiles": tiles, "dest": dest, "outside": outside, "cotangent": cotangent}


def reference(features, w_self, w_neigh, tiles, dest, outside, cotangent):
    self_part = jnp.dot(features, w_self, preferred_element_type=jnp.float32)
    message = jnp.dot(features, w_neigh, preferred_element_type=jnp.float32).astype(jnp.bfloat16)
    msg_blocks = message.reshape(N_DOM, BLOCK, HID)
    tile_groups = tiles.reshape(N_DOM, TILES_DEV, BLOCK, BLOCK)
    dest_groups = dest.reshape(N_DOM, TILES_DEV).astype(jnp.int32)

    def forward_step(carry, inputs):
        total, link_total = carry
        group, targets, block_rows = inputs
        group_f = group.astype(jnp.float32)
        partial_sum = jnp.einsum("tij,ik->tjk", group_f, block_rows.astype(jnp.float32))
        column_sums = jnp.sum(group_f, axis=1)
        return (total.at[targets].add(partial_sum), link_total.at[targets].add(column_sums)), None

    start = (jnp.zeros((N_DOM, BLOCK, HID), jnp.float32), jnp.zeros((N_DOM, BLOCK), jnp.float32))
    (summed, links), _ = lax.scan(forward_step, start, (tile_groups, dest_groups, msg_blocks))
    inverse = 1.0 / (links.reshape(NODES) + outside.astype(jnp.float32))
    pre = self_part + summed.reshape(NODES, HID) * inverse[:, None]
    sigma = jax.nn.sigmoid(pre)
    output = (pre * sigma).astype(jnp.bfloat16)
    dpre = (cotangent.astype(jnp.float32) * sigma * (1.0 + pre * (1.0 - sigma))).astype(jnp.bfloat16)
    dagg = (dpre.astype(jnp.float32) * inverse[:, None]).astype(jnp.bfloat16)
    dagg_blocks = dagg.reshape(N_DOM, BLOCK, HID)

    def backward_step(carry, inputs):
        group, targets = inputs
        fetched = dagg_blocks[targets]
        return carry, jnp.einsum("tij,tjk->ik", group.astype(jnp.float32), fetched.astype(jnp.float32))

    _, dmessage = lax.scan(backward_step, jnp.float32(0.0), (tile_groups, dest_groups))
    dmessage = dmessage.reshape(NODES, HID).astype(jnp.bfloat16)
    grad_self = jnp.dot(features.T, dpre, preferred_element_type=jnp.float32)
    grad_neigh = jnp.dot(features.T, dmessage, preferred_element_type=jnp.float32)
    grad_input = (jnp.dot(dpre, w_self.T, preferred_element_type=jnp.float32) + jnp.dot(dmessage, w_neigh.T, preferred_element_type=jnp.float32)).astype(jnp.bfloat16)
    return output, grad_input, grad_self, grad_neigh
```

```python
import jax
import jax.numpy as jnp
from jax import lax
from jax.experimental import pallas as pl
from jax.experimental.pallas import tpu as pltpu
from jax.sharding import PartitionSpec as P

MESH = pl.DeviceIdType.MESH
BF = jnp.bfloat16
F32 = jnp.float32
NX, NY, NZ = 4, 4, 8
B = 128
SPREAD = (2, 1, 3)


def far_first(p):
    half = (p + 1) // 2
    return 4 + half * (1 - 2 * (p % 2))


def kernel(
    feat_h, ws_h, wn_h, tiles_h, dest_h, outside_h, cot_h,
    out_h, gi_h, gs_h, gn_h,
    feat, ws, wn, dest, outside, cot, out_o, gi_o,
    tiles, adj, xt, idx_v, idx_s, selfp,
    sx, sy, r1x, r1y, p1x, p1y, r2x, r2y, p2x, p2y, r3,
    lk, rlk1, plk, rlk2, lk2, rlk3,
    gpart, grecv, gx, gy,
    w0, rw1, w1, rw2, rw3, wg, gis, gir,
    load_sem, s1, rs1x, rs1y, s2, rs2, s3, rs3, sl, rsl, sg, rsg,
    sa, ra, sb, rbx, rby, sc, rcx, rcy, sw, rw, out_sem,
):
    dom = lax.axis_index("dom")
    c = lax.axis_index("feat")
    x = lax.rem(dom, NX)
    z = lax.rem(dom // NX, NZ)
    y = dom // (NX * NZ)
    oc = 1 - c

    def dev(px, py, pz, pc):
        return ((py * NZ + pz) * NX + px, pc)

    def xp(k):
        return lax.rem(x + k, NX)

    def yp(k):
        return lax.rem(y + k, NY)

    def zp(k):
        return lax.rem(z + k, NZ)

    def push(src, dst, send, recv, device):
        pltpu.make_async_remote_copy(
            src_ref=src, dst_ref=dst, send_sem=send, recv_sem=recv,
            device_id=device, device_id_type=MESH,
        ).start()

    def take(ref, sem):
        pltpu.make_async_copy(ref, ref, sem).wait()

    loads = [
        pltpu.make_async_copy(src, dst, load_sem.at[i])
        for i, (src, dst) in enumerate(
            (
                (dest_h, dest), (tiles_h, tiles.at[pl.ds(0, B)]), (feat_h, feat), (ws_h, ws),
                (wn_h, wn), (cot_h, cot), (outside_h, outside),
            )
        )
    ]
    for load in loads:
        load.start()

    barrier = pltpu.get_barrier_semaphore()
    greeted = 0
    for pc in (c, oc):
        for k in (1, 2, 3):
            for d in (dev(xp(k), y, z, pc), dev(x, yp(k), z, pc)):
                pl.semaphore_signal(barrier, inc=1, device_id=d, device_id_type=MESH)
                greeted += 1
    for k in range(1, NZ):
        pl.semaphore_signal(barrier, inc=1, device_id=dev(x, y, zp(k), c), device_id_type=MESH)
        greeted += 1
    pl.semaphore_signal(barrier, inc=1, device_id=dev(x, y, z, oc), device_id_type=MESH)
    greeted += 1

    loads[0].wait()
    named = jnp.broadcast_to(dest[...], (B, B)).T
    lanes = lax.broadcasted_iota(jnp.int32, (B, B), 1)
    rows = lax.broadcasted_iota(jnp.int32, (B, B), 0)
    hit = named == lanes
    last = jnp.max(jnp.where(hit, rows, -1), axis=0, keepdims=True)
    first = jnp.min(jnp.where(hit, rows, B), axis=0, keepdims=True)
    idx_v[0:1, :] = first
    idx_v[1:2, :] = jnp.where(last > first, last, B)
    table = pltpu.make_async_copy(idx_v, idx_s, load_sem.at[7])
    table.start()
    tiles[B] = jnp.zeros((B, B), BF)
    loads[2].wait()
    features = feat[...]
    xt[0:B, :] = features.astype(F32).T.astype(BF)
    xh = xt[pl.ds(pl.multiple_of(c * 64, 64), 64), :]
    left = jnp.concatenate([xh, jnp.ones((16, B), BF)], axis=0)
    loads[3].wait()
    selfp[...] = jnp.dot(features, ws[...], preferred_element_type=F32)
    lk[...] = jnp.zeros_like(lk)
    table.wait()
    loads[1].wait()
    pl.semaphore_wait(barrier, greeted)

    def first_phase(p, carry):
        dz = zp(far_first(p))
        for py in range(NY):
            parts = []
            for px in range(NX):
                d = (py * NZ + dz) * NX + px
                both = tiles[idx_s[0, d]] + tiles[idx_s[1, d]]
                adj[p, py, :, px * B:(px + 1) * B] = both
                parts.append(both)
            o = jnp.dot(left, jnp.concatenate(parts, axis=1), preferred_element_type=F32)
            for px in range(NX):
                part = o[:, px * B:(px + 1) * B]
                sx[p, px, py] = part[0:32].astype(BF)
                sy[p, py, px] = part[32:64].astype(BF)
                lk[px, p, py:py + 1, :] = part[64:65]
        for k in SPREAD:
            push(sx.at[p, xp(k)], r1x.at[p, k - 1], s1.at[0], rs1x.at[p], dev(xp(k), y, z, c))
            push(sy.at[p, yp(k)], r1y.at[p, k - 1], s1.at[1], rs1y.at[p], dev(x, yp(k), z, c))
        return carry

    lax.fori_loop(0, NZ, first_phase, 0)
    for k in SPREAD:
        push(lk.at[xp(k)], rlk1.at[k - 1], sl.at[0], rsl.at[0], dev(xp(k), y, z, c))

    def add_four(own, got):
        total = own.astype(F32)
        for k in range(3):
            total = total + got[k].astype(F32)
        return total

    def second_phase(p, carry):
        to = dev(x, y, zp(far_first(p)), c)
        take(r1x.at[p], rs1x.at[p])
        p1x[p] = add_four(sx[p, x], r1x.at[p]).astype(BF)
        push(p1x.at[p], r2x.at[p], s2.at[0], rs2.at[0], to)
        take(r1y.at[p], rs1y.at[p])
        p1y[p] = add_four(sy[p, y], r1y.at[p]).astype(BF)
        push(p1y.at[p], r2y.at[p], s2.at[1], rs2.at[1], to)
        return carry

    lax.fori_loop(0, NZ - 1, second_phase, 0)
    take(rlk1, rsl.at[0])
    plk[...] = lk[x] + rlk1[0] + rlk1[1] + rlk1[2]
    for p in range(NZ - 1):
        push(plk.at[p], rlk2.at[p], sl.at[1], rsl.at[1], dev(x, y, zp(far_first(p)), c))
    own = NZ - 1
    take(r1x.at[own], rs1x.at[own])
    keep_x = add_four(sx[own, x], r1x.at[own])
    take(r1y.at[own], rs1y.at[own])
    keep_y = add_four(sy[own, y], r1y.at[own])

    take(r2x, rs2.at[0])
    for p in range(NZ - 1):
        keep_x = keep_x + r2x[p].astype(F32)
    p2x[...] = keep_x.astype(BF)
    for pc in (c, oc):
        for k in SPREAD:
            push(p2x.at[yp(k)], r3.at[c * 4 + k], s3, rs3, dev(x, yp(k), z, pc))
    push(p2x.at[y], r3.at[c * 4], s3, rs3, dev(x, y, z, oc))
    take(r2y, rs2.at[1])
    for p in range(NZ - 1):
        keep_y = keep_y + r2y[p].astype(F32)
    p2y[...] = keep_y.astype(BF)
    for pc in (c, oc):
        for k in SPREAD:
            push(p2y.at[xp(k)], r3.at[8 + c * 4 + k], s3, rs3, dev(xp(k), y, z, pc))
    push(p2y.at[x], r3.at[8 + c * 4], s3, rs3, dev(x, y, z, oc))
    take(rlk2, rsl.at[1])
    total = plk[own]
    for p in range(NZ - 1):
        total = total + rlk2[p]
    lk2[...] = total
    for k in SPREAD:
        push(lk2, rlk3.at[k - 1], sl.at[2], rsl.at[2], dev(x, yp(k), z, c))
    r3[c * 4] = p2x[y]
    r3[8 + c * 4] = p2y[x]
    loads[6].wait()
    take(rlk3, rsl.at[2])
    links = lk2[pl.ds(y, 1), :]
    for k in range(3):
        links = links + rlk3[k, pl.ds(y, 1), :]
    inverse = 1.0 / (links + outside[...].astype(F32))
    take(r3.at[pl.ds(0, 14)], rs3)
    pieces = []
    for pc in range(2):
        for share in range(2):
            slot = share * 8 + pc * 4
            piece = r3[slot].astype(F32)
            for k in range(1, 4):
                piece = piece + r3[slot + k].astype(F32)
            pieces.append(piece)
    mean_t = jnp.concatenate(pieces, axis=0) * inverse
    mean_tb = mean_t.astype(BF)

    loads[4].wait()
    loads[5].wait()
    pre = selfp[...] + jnp.dot(mean_t.T.astype(BF), wn[...], preferred_element_type=F32)
    sigma = jax.nn.sigmoid(pre)
    out_o[...] = (pre * sigma).astype(BF)
    emit = [pltpu.make_async_copy(out_o, out_h, out_sem.at[0])]
    emit[0].start()
    dpre = (cot[...].astype(F32) * sigma * (1.0 + pre * (1.0 - sigma))).astype(BF)
    across = (((1,), (1,)), ((), ()))
    gpart[...] = lax.dot_general(wn[...], dpre, across, preferred_element_type=F32) * inverse
    push(gpart.at[pl.ds(pl.multiple_of(oc * 64, 64), 64)], grecv, sg.at[0], rsg.at[0], dev(x, y, z, oc))
    grad_s = jnp.dot(xt[...], dpre, preferred_element_type=F32)
    grad_n = jnp.dot(mean_tb, dpre, preferred_element_type=F32)
    for k in range(2):
        w0[k] = grad_s[64 * k:64 * k + 64]
        w0[k + 2] = grad_n[64 * k:64 * k + 64]
    direct = lax.dot_general(dpre, ws[...], across, preferred_element_type=F32)
    take(grecv, rsg.at[0])
    gfull = (gpart[pl.ds(pl.multiple_of(c * 64, 64), 64), :] + grecv[...]).astype(BF)
    gx[0, x, y] = gfull[0:32]
    gy[0, y, x] = gfull[32:64]

    for k in SPREAD:
        push(gx.at[0, x, y], gx.at[0, x, y], sa.at[0], ra.at[0], dev(x, yp(k), z, c))
        push(gy.at[0, y, x], gy.at[0, y, x], sa.at[1], ra.at[1], dev(xp(k), y, z, c))
    for k in SPREAD:
        push(w0.at[xp(k)], rw1.at[k - 1], sw.at[0], rw.at[0], dev(xp(k), y, z, c))

    near = (0, 7, 1, 6, 2, 5, 3, 4)
    take(gx.at[0, x, pl.ds(0, 3)], ra.at[0])
    for q in range(1, NZ):
        push(gx.at[0, x], gx.at[q, x], sb.at[0], rbx.at[q], dev(x, y, zp(NZ - near[q]), c))
    take(gy.at[0, y, pl.ds(0, 3)], ra.at[1])
    for q in range(1, NZ):
        push(gy.at[0, y], gy.at[q, y], sb.at[1], rby.at[q], dev(x, y, zp(NZ - near[q]), c))

    def forward(q):
        if q > 0:
            take(gx.at[q, x], rbx.at[q])
        for k in SPREAD:
            push(gx.at[q, x], gx.at[q, x], sc.at[0], rcx.at[q], dev(xp(k), y, z, c))
        if q > 0:
            take(gy.at[q, y], rby.at[q])
        for k in SPREAD:
            push(gy.at[q, y], gy.at[q, y], sc.at[1], rcy.at[q], dev(x, yp(k), z, c))

    for q in range(0, 3):
        forward(q)
    take(rw1, rw.at[0])
    w1[...] = (w0[x] + rw1[0] + rw1[1] + rw1[2]).reshape(4, 16, B)
    for k in SPREAD:
        push(w1.at[yp(k)], rw2.at[k - 1], sw.at[1], rw.at[1], dev(x, yp(k), z, c))
    for q in range(3, NZ):
        forward(q)
    take(rw2, rw.at[1])
    rw3[z] = w1[y] + rw2[0] + rw2[1] + rw2[2]
    for k in range(1, NZ):
        push(rw3.at[z], rw3.at[z], sw.at[2], rw.at[2], dev(x, y, zp(k), c))

    def last_phase(q, acc):
        take(gx.at[q, pl.ds(0, 3)], rcx.at[q])
        take(gy.at[q, pl.ds(0, 3)], rcy.at[q])
        for py in range(NY):
            right = jnp.concatenate(
                [jnp.concatenate([gx[q, px, py], gy[q, py, px]], axis=0) for px in range(NX)], axis=1
            )
            acc = acc + lax.dot_general(adj[NZ - 1 - q, py], right, across, preferred_element_type=F32)
        return acc

    acc = lax.fori_loop(0, 3, last_phase, jnp.zeros((B, 64), F32))
    take(rw3.at[pl.ds(0, 7)], rw.at[2])
    total = rw3[0]
    for k in range(1, NZ):
        total = total + rw3[k]
    wg[x, y] = total
    for k in SPREAD:
        push(wg.at[x, y], wg.at[x, y], sw.at[3], rw.at[3], dev(x, yp(k), z, c))
    acc = lax.fori_loop(3, 6, last_phase, acc)
    take(wg.at[x, pl.ds(0, 3)], rw.at[3])
    for k in SPREAD:
        push(wg.at[x], wg.at[x], sw.at[4], rw.at[4], dev(xp(k), y, z, c))
    acc = lax.fori_loop(6, 8, last_phase, acc)

    none = jnp.zeros((B, 64), F32)
    placed = jnp.where(c == 0, jnp.concatenate([acc, none], axis=1), jnp.concatenate([none, acc], axis=1))
    gis[...] = placed + direct
    push(gis, gir, sg.at[1], rsg.at[1], dev(x, y, z, oc))
    take(wg.at[pl.ds(0, 3)], rw.at[4])
    emit.append(pltpu.make_async_copy(wg.at[pl.ds(0, 2)], gs_h, out_sem.at[1]))
    emit.append(pltpu.make_async_copy(wg.at[pl.ds(2, 2)], gn_h, out_sem.at[2]))
    emit[1].start()
    emit[2].start()

    take(sx.at[:, pl.ds(0, 3)], s1.at[0])
    take(sy.at[:, pl.ds(0, 3)], s1.at[1])
    take(lk.at[pl.ds(0, 3)], sl.at[0])
    take(p1x.at[pl.ds(0, 7)], s2.at[0])
    take(p1y.at[pl.ds(0, 7)], s2.at[1])
    take(plk.at[pl.ds(0, 7)], sl.at[1])
    take(r3.at[pl.ds(0, 14)], s3)
    take(rlk3, sl.at[2])
    take(grecv, sg.at[0])
    take(gx.at[0, 0, pl.ds(0, 3)], sa.at[0])
    take(gy.at[0, 0, pl.ds(0, 3)], sa.at[1])
    take(gx.at[pl.ds(0, 7), 0], sb.at[0])
    take(gy.at[pl.ds(0, 7), 0], sb.at[1])
    take(gx.at[:, pl.ds(0, 3)], sc.at[0])
    take(gy.at[:, pl.ds(0, 3)], sc.at[1])
    take(rw1, sw.at[0])
    take(rw2, sw.at[1])
    take(rw3.at[pl.ds(0, 7)], sw.at[2])
    take(wg.at[0, pl.ds(0, 3)], sw.at[3])
    take(wg.at[pl.ds(0, 3)], sw.at[4])
    take(gir, rsg.at[1])
    gi_o[...] = (gis[...] + gir[...]).astype(BF)
    emit.append(pltpu.make_async_copy(gi_o, gi_h, out_sem.at[3]))
    emit[3].start()
    take(gis, sg.at[1])
    for copy in emit:
        copy.wait()


def hand_out(a, b, d, e, ao, bo, do, eo, sems):
    copies = [
        pltpu.make_async_copy(src, dst, sems.at[i])
        for i, (src, dst) in enumerate(((a, ao), (b, bo), (d, do), (e, eo)))
    ]
    for copy in copies:
        copy.start()
    for copy in copies:
        copy.wait()


def on_device(features, w_self, w_neigh, tiles, dest, outside, cotangent):
    hbm = pl.BlockSpec(memory_space=pltpu.HBM)
    dma = pltpu.SemaphoreType.DMA
    V = pltpu.VMEM
    results = pl.pallas_call(
        kernel,
        out_shape=(
            jax.ShapeDtypeStruct((B, B), BF),
            jax.ShapeDtypeStruct((B, B), BF),
            jax.ShapeDtypeStruct((2, NY, 16, B), F32),
            jax.ShapeDtypeStruct((2, NY, 16, B), F32),
        ),
        in_specs=[hbm] * 7,
        out_specs=(hbm,) * 4,
        scratch_shapes=[
            V((B, B), BF), V((B, B), BF), V((B, B), BF), V((1, B), jnp.int32), V((1, B), jnp.int32),
            V((B, B), BF), V((B, B), BF), V((B, B), BF),
            V((B + 1, B, B), BF),
            V((NZ, NY, B, NX * B), BF),
            V((B, B), BF),
            V((8, B), jnp.int32),
            pltpu.SMEM((8, B), jnp.int32),
            V((B, B), F32),
            V((NZ, NX, NY, 32, B), BF),
            V((NZ, NY, NX, 32, B), BF),
            V((NZ, 3, NY, 32, B), BF),
            V((NZ, 3, NX, 32, B), BF),
            V((NZ, NY, 32, B), BF),
            V((NZ, NX, 32, B), BF),
            V((NZ - 1, NY, 32, B), BF),
            V((NZ - 1, NX, 32, B), BF),
            V((NY, 32, B), BF),
            V((NX, 32, B), BF),
            V((16, 32, B), BF),
            V((NX, NZ, 8, B), F32),
            V((3, NZ, 8, B), F32),
            V((NZ, 8, B), F32),
            V((NZ - 1, 8, B), F32),
            V((8, B), F32),
            V((3, 8, B), F32),
            V((B, B), F32),
            V((64, B), F32),
            V((NZ, NX, NY, 32, B), BF),
            V((NZ, NY, NX, 32, B), BF),
            V((4, 64, B), F32),
            V((3, 64, B), F32),
            V((4, 16, B), F32),
            V((3, 16, B), F32),
            V((NZ, 16, B), F32),
            V((NX, NY, 16, B), F32),
            V((B, B), F32),
            V((B, B), F32),
            dma((8,)),
            dma((2,)), dma((NZ,)), dma((NZ,)),
            dma((2,)), dma((2,)),
            dma(()), dma(()),
            dma((3,)), dma((3,)),
            dma((2,)), dma((2,)),
            dma((2,)), dma((2,)),
            dma((2,)), dma((NZ,)), dma((NZ,)),
            dma((2,)), dma((NZ,)), dma((NZ,)),
            dma((5,)), dma((5,)),
            dma((4,)),
        ],
        compiler_params=pltpu.CompilerParams(
            collective_id=0, has_side_effects=True, vmem_limit_bytes=60 * 2**20
        ),
        name="sage",
    )(features, w_self, w_neigh, tiles, dest.reshape(1, B), outside.reshape(1, B), cotangent)
    results = pl.pallas_call(
        hand_out,
        out_shape=tuple(jax.ShapeDtypeStruct(r.shape, r.dtype) for r in results),
        in_specs=[hbm] * 4,
        out_specs=(hbm,) * 4,
        scratch_shapes=[dma((4,))],
        name="hand_out",
    )(*results)
    output, grad_input, grad_self, grad_neigh = results
    return output, grad_input, grad_self.reshape(B, B), grad_neigh.reshape(B, B)


def solution(mesh):
    placed = (
        P("dom", None),
        P(None, "feat"),
        P(None, "feat"),
        P("dom", None, None),
        P("dom", None),
        P("dom"),
        P("dom", "feat"),
    )
    return jax.shard_map(
        on_device,
        mesh=mesh,
        in_specs=placed,
        out_specs=(P("dom", "feat"), P("dom", None), P(None, "feat"), P(None, "feat")),
        check_vma=False,
    )
```

```python
import jax
import jax.numpy as jnp
from jax import lax
from jax.experimental import pallas as pl
from jax.experimental.pallas import tpu as pltpu
from jax.sharding import PartitionSpec as P

MESH = pl.DeviceIdType.MESH
BF = jnp.bfloat16
F32 = jnp.float32
NX, NY, NZ = 4, 4, 8
B = 128
SPREAD = (2, 1, 3)


def far_first(p):
    half = (p + 1) // 2
    return 4 + half * (1 - 2 * (p % 2))


def kernel(
    feat_h, ws_h, wn_h, tiles_h, dest_h, outside_h, cot_h,
    out_h, gi_h, gs_h, gn_h,
    feat, ws, wn, dest, outside, cot, out_o, gi_o,
    tiles, adj, xt, idx_v, idx_s, selfp,
    sx, sy, r1x, r1y, p1x, p1y, r2x, r2y, p2x, p2y, r3,
    lk, rlk1, plk, rlk2, lk2, rlk3,
    gpart, grecv, gx, gy,
    w0, rw1, w1, rw2, rw3, wg, gis, gir,
    load_sem, s1, rs1x, rs1y, s2, rs2, s3, rs3, sl, rsl, sg, rsg,
    sa, ra, sb, rbx, rby, sc, rcx, rcy, sw, rw, out_sem,
):
    dom = lax.axis_index("dom")
    c = lax.axis_index("feat")
    x = lax.rem(dom, NX)
    z = lax.rem(dom // NX, NZ)
    y = dom // (NX * NZ)
    oc = 1 - c

    def dev(px, py, pz, pc):
        return ((py * NZ + pz) * NX + px, pc)

    def xp(k):
        return lax.rem(x + k, NX)

    def yp(k):
        return lax.rem(y + k, NY)

    def zp(k):
        return lax.rem(z + k, NZ)

    def push(src, dst, send, recv, device):
        pltpu.make_async_remote_copy(
            src_ref=src, dst_ref=dst, send_sem=send, recv_sem=recv,
            device_id=device, device_id_type=MESH,
        ).start()

    def take(ref, sem):
        pltpu.make_async_copy(ref, ref, sem).wait()

    debts = []

    def owe(ref, sem):
        debts.append((ref, sem))

    def settle():
        for ref, sem in debts:
            take(ref, sem)

    loads = [
        pltpu.make_async_copy(src, dst, load_sem.at[i])
        for i, (src, dst) in enumerate(
            (
                (dest_h, dest), (tiles_h, tiles.at[pl.ds(0, B)]), (feat_h, feat), (ws_h, ws),
                (wn_h, wn), (cot_h, cot), (outside_h, outside),
            )
        )
    ]
    for load in loads:
        load.start()

    barrier = pltpu.get_barrier_semaphore()
    greeted = 0
    for pc in (c, oc):
        for k in (1, 2, 3):
            for d in (dev(xp(k), y, z, pc), dev(x, yp(k), z, pc)):
                pl.semaphore_signal(barrier, inc=1, device_id=d, device_id_type=MESH)
                greeted += 1
    for k in range(1, NZ):
        pl.semaphore_signal(barrier, inc=1, device_id=dev(x, y, zp(k), c), device_id_type=MESH)
        greeted += 1
    pl.semaphore_signal(barrier, inc=1, device_id=dev(x, y, z, oc), device_id_type=MESH)
    greeted += 1

    loads[0].wait()
    named = jnp.broadcast_to(dest[...], (B, B)).T
    lanes = lax.broadcasted_iota(jnp.int32, (B, B), 1)
    rows = lax.broadcasted_iota(jnp.int32, (B, B), 0)
    hit = named == lanes
    last = jnp.max(jnp.where(hit, rows, -1), axis=0, keepdims=True)
    first = jnp.min(jnp.where(hit, rows, B), axis=0, keepdims=True)
    idx_v[0:1, :] = first
    idx_v[1:2, :] = jnp.where(last > first, last, B)
    table = pltpu.make_async_copy(idx_v, idx_s, load_sem.at[7])
    table.start()
    tiles[B] = jnp.zeros((B, B), BF)
    loads[2].wait()
    features = feat[...]
    xt[0:B, :] = features.astype(F32).T.astype(BF)
    xh = xt[pl.ds(pl.multiple_of(c * 64, 64), 64), :]
    left = jnp.concatenate([xh, jnp.ones((16, B), BF)], axis=0)
    loads[3].wait()
    selfp[...] = jnp.dot(features, ws[...], preferred_element_type=F32)
    lk[...] = jnp.zeros_like(lk)
    table.wait()
    loads[1].wait()
    pl.semaphore_wait(barrier, greeted)

    def first_phase(p, carry):
        dz = zp(far_first(p))
        for py in range(NY):
            parts = []
            for px in range(NX):
                d = (py * NZ + dz) * NX + px
                both = tiles[idx_s[0, d]] + tiles[idx_s[1, d]]
                adj[p, py, :, px * B:(px + 1) * B] = both
                parts.append(both)
            o = jnp.dot(left, jnp.concatenate(parts, axis=1), preferred_element_type=F32)
            for px in range(NX):
                part = o[:, px * B:(px + 1) * B]
                sx[p, px, py] = part[0:32].astype(BF)
                sy[p, py, px] = part[32:64].astype(BF)
                lk[px, p, py:py + 1, :] = part[64:65]
        for k in SPREAD:
            push(sx.at[p, xp(k)], r1x.at[p, k - 1], s1.at[0], rs1x.at[p], dev(xp(k), y, z, c))
            push(sy.at[p, yp(k)], r1y.at[p, k - 1], s1.at[1], rs1y.at[p], dev(x, yp(k), z, c))
        return carry

    lax.fori_loop(0, NZ, first_phase, 0)
    owe(sx.at[:, pl.ds(0, 3)], s1.at[0])
    owe(sy.at[:, pl.ds(0, 3)], s1.at[1])
    owe(lk.at[pl.ds(0, 3)], sl.at[0])
    for k in SPREAD:
        push(lk.at[xp(k)], rlk1.at[k - 1], sl.at[0], rsl.at[0], dev(xp(k), y, z, c))

    def add_four(own, got):
        total = own.astype(F32)
        for k in range(3):
            total = total + got[k].astype(F32)
        return total

    def second_phase(p, carry):
        to = dev(x, y, zp(far_first(p)), c)
        take(r1x.at[p], rs1x.at[p])
        p1x[p] = add_four(sx[p, x], r1x.at[p]).astype(BF)
        push(p1x.at[p], r2x.at[p], s2.at[0], rs2.at[0], to)
        take(r1y.at[p], rs1y.at[p])
        p1y[p] = add_four(sy[p, y], r1y.at[p]).astype(BF)
        push(p1y.at[p], r2y.at[p], s2.at[1], rs2.at[1], to)
        return carry

    lax.fori_loop(0, NZ - 1, second_phase, 0)
    owe(p1x.at[pl.ds(0, 7)], s2.at[0])
    owe(p1y.at[pl.ds(0, 7)], s2.at[1])
    owe(plk.at[pl.ds(0, 7)], sl.at[1])
    take(rlk1, rsl.at[0])
    plk[...] = lk[x] + rlk1[0] + rlk1[1] + rlk1[2]
    for p in range(NZ - 1):
        push(plk.at[p], rlk2.at[p], sl.at[1], rsl.at[1], dev(x, y, zp(far_first(p)), c))
    own = NZ - 1
    take(r1x.at[own], rs1x.at[own])
    keep_x = add_four(sx[own, x], r1x.at[own])
    take(r1y.at[own], rs1y.at[own])
    keep_y = add_four(sy[own, y], r1y.at[own])

    take(r2x, rs2.at[0])
    for p in range(NZ - 1):
        keep_x = keep_x + r2x[p].astype(F32)
    p2x[...] = keep_x.astype(BF)
    for pc in (c, oc):
        for k in SPREAD:
            push(p2x.at[yp(k)], r3.at[c * 4 + k], s3, rs3, dev(x, yp(k), z, pc))
    push(p2x.at[y], r3.at[c * 4], s3, rs3, dev(x, y, z, oc))
    take(r2y, rs2.at[1])
    for p in range(NZ - 1):
        keep_y = keep_y + r2y[p].astype(F32)
    p2y[...] = keep_y.astype(BF)
    for pc in (c, oc):
        for k in SPREAD:
            push(p2y.at[xp(k)], r3.at[8 + c * 4 + k], s3, rs3, dev(xp(k), y, z, pc))
    push(p2y.at[x], r3.at[8 + c * 4], s3, rs3, dev(x, y, z, oc))
    take(rlk2, rsl.at[1])
    total = plk[own]
    for p in range(NZ - 1):
        total = total + rlk2[p]
    lk2[...] = total
    for k in SPREAD:
        push(lk2, rlk3.at[k - 1], sl.at[2], rsl.at[2], dev(x, yp(k), z, c))
    r3[c * 4] = p2x[y]
    r3[8 + c * 4] = p2y[x]
    owe(r3.at[pl.ds(0, 14)], s3)
    owe(rlk3, sl.at[2])
    loads[6].wait()
    take(rlk3, rsl.at[2])
    links = lk2[pl.ds(y, 1), :]
    for k in range(3):
        links = links + rlk3[k, pl.ds(y, 1), :]
    inverse = 1.0 / (links + outside[...].astype(F32))
    take(r3.at[pl.ds(0, 14)], rs3)
    pieces = []
    for pc in range(2):
        for share in range(2):
            slot = share * 8 + pc * 4
            piece = r3[slot].astype(F32)
            for k in range(1, 4):
                piece = piece + r3[slot + k].astype(F32)
            pieces.append(piece)
    mean_t = jnp.concatenate(pieces, axis=0) * inverse
    mean_tb = mean_t.astype(BF)

    loads[4].wait()
    loads[5].wait()
    pre = selfp[...] + jnp.dot(mean_t.T.astype(BF), wn[...], preferred_element_type=F32)
    sigma = jax.nn.sigmoid(pre)
    out_o[...] = (pre * sigma).astype(BF)
    emit = [pltpu.make_async_copy(out_o, out_h, out_sem.at[0])]
    emit[0].start()
    dpre = (cot[...].astype(F32) * sigma * (1.0 + pre * (1.0 - sigma))).astype(BF)
    across = (((1,), (1,)), ((), ()))
    gpart[...] = lax.dot_general(wn[...], dpre, across, preferred_element_type=F32) * inverse
    push(gpart.at[pl.ds(pl.multiple_of(oc * 64, 64), 64)], grecv, sg.at[0], rsg.at[0], dev(x, y, z, oc))
    owe(grecv, sg.at[0])
    grad_s = jnp.dot(xt[...], dpre, preferred_element_type=F32)
    grad_n = jnp.dot(mean_tb, dpre, preferred_element_type=F32)
    for k in range(2):
        w0[k] = grad_s[64 * k:64 * k + 64]
        w0[k + 2] = grad_n[64 * k:64 * k + 64]
    for k in SPREAD:
        push(w0.at[xp(k)], rw1.at[k - 1], sw.at[0], rw.at[0], dev(xp(k), y, z, c))
    owe(rw1, sw.at[0])
    direct = lax.dot_general(dpre, ws[...], across, preferred_element_type=F32)
    take(grecv, rsg.at[0])
    gfull = (gpart[pl.ds(pl.multiple_of(c * 64, 64), 64), :] + grecv[...]).astype(BF)
    gx[0, x, y] = gfull[0:32]
    gy[0, y, x] = gfull[32:64]

    near = (0, 7, 1, 6, 2, 5, 3, 4)
    for q in range(1, NZ):
        to = dev(x, y, zp(NZ - near[q]), c)
        push(gx.at[0, x, y], gx.at[q, x, y], sa.at[0], ra.at[q], to)
        push(gy.at[0, y, x], gy.at[q, y, x], sa.at[1], ra.at[q], to)
    owe(gx.at[0, 0, pl.ds(0, 4)], sa.at[0])
    owe(gx.at[0, 0, pl.ds(0, 3)], sa.at[0])
    owe(gy.at[0, 0, pl.ds(0, 4)], sa.at[1])
    owe(gy.at[0, 0, pl.ds(0, 3)], sa.at[1])

    def across_second(q):
        if q > 0:
            take(gx.at[q, x, pl.ds(0, 2)], ra.at[q])
        for k in SPREAD:
            push(gx.at[q, x, y], gx.at[q, x, y], sb.at[0], rbx.at[q], dev(x, yp(k), z, c))
            push(gy.at[q, y, x], gy.at[q, y, x], sb.at[1], rby.at[q], dev(xp(k), y, z, c))

    def across_third(q):
        take(gx.at[q, x, pl.ds(0, 3)], rbx.at[q])
        for k in SPREAD:
            push(gx.at[q, x], gx.at[q, x], sc.at[0], rcx.at[q], dev(xp(k), y, z, c))
        take(gy.at[q, y, pl.ds(0, 3)], rby.at[q])
        for k in SPREAD:
            push(gy.at[q, y], gy.at[q, y], sc.at[1], rcy.at[q], dev(x, yp(k), z, c))

    across_second(0)
    across_second(1)
    across_second(2)
    across_third(0)
    take(rw1, rw.at[0])
    w1[...] = (w0[x] + rw1[0] + rw1[1] + rw1[2]).reshape(4, 16, B)
    for k in SPREAD:
        push(w1.at[yp(k)], rw2.at[k - 1], sw.at[1], rw.at[1], dev(x, yp(k), z, c))
    owe(rw2, sw.at[1])
    across_second(3)
    across_second(4)
    across_third(1)
    across_third(2)
    across_second(5)
    across_second(6)
    take(rw2, rw.at[1])
    rw3[z] = w1[y] + rw2[0] + rw2[1] + rw2[2]
    for k in range(1, NZ):
        push(rw3.at[z], rw3.at[z], sw.at[2], rw.at[2], dev(x, y, zp(k), c))
    owe(rw3.at[pl.ds(0, 7)], sw.at[2])
    across_third(3)
    across_third(4)
    across_second(7)
    across_third(5)
    across_third(6)
    across_third(7)
    owe(gx.at[:, 0, pl.ds(0, 3)], sb.at[0])
    owe(gy.at[:, 0, pl.ds(0, 3)], sb.at[1])
    owe(gx.at[:, pl.ds(0, 3)], sc.at[0])
    owe(gy.at[:, pl.ds(0, 3)], sc.at[1])

    def last_phase(q, acc):
        take(gx.at[q, pl.ds(0, 3)], rcx.at[q])
        take(gy.at[q, pl.ds(0, 3)], rcy.at[q])
        for py in range(NY):
            right = jnp.concatenate(
                [jnp.concatenate([gx[q, px, py], gy[q, py, px]], axis=0) for px in range(NX)], axis=1
            )
            acc = acc + lax.dot_general(adj[NZ - 1 - q, py], right, across, preferred_element_type=F32)
        return acc

    take(rw3.at[pl.ds(0, 7)], rw.at[2])
    total = rw3[0]
    for k in range(1, NZ):
        total = total + rw3[k]
    wg[x, y] = total
    for k in SPREAD:
        push(wg.at[x, y], wg.at[x, y], sw.at[3], rw.at[3], dev(x, yp(k), z, c))
    acc = lax.fori_loop(0, 3, last_phase, jnp.zeros((B, 64), F32))
    take(wg.at[x, pl.ds(0, 3)], rw.at[3])
    for k in SPREAD:
        push(wg.at[x], wg.at[x], sw.at[4], rw.at[4], dev(xp(k), y, z, c))
    acc = lax.fori_loop(3, 8, last_phase, acc)

    owe(wg.at[0, pl.ds(0, 3)], sw.at[3])
    owe(wg.at[pl.ds(0, 3)], sw.at[4])
    none = jnp.zeros((B, 64), F32)
    placed = jnp.where(c == 0, jnp.concatenate([acc, none], axis=1), jnp.concatenate([none, acc], axis=1))
    gis[...] = placed + direct
    push(gis, gir, sg.at[1], rsg.at[1], dev(x, y, z, oc))
    take(wg.at[pl.ds(0, 3)], rw.at[4])
    emit.append(pltpu.make_async_copy(wg.at[pl.ds(0, 2)], gs_h, out_sem.at[1]))
    emit.append(pltpu.make_async_copy(wg.at[pl.ds(2, 2)], gn_h, out_sem.at[2]))
    emit[1].start()
    emit[2].start()

    settle()
    take(gir, rsg.at[1])
    gi_o[...] = (gis[...] + gir[...]).astype(BF)
    emit.append(pltpu.make_async_copy(gi_o, gi_h, out_sem.at[3]))
    emit[3].start()
    take(gis, sg.at[1])
    for copy in emit:
        copy.wait()


def hand_out(*refs):
    sources, targets, held, sems = refs[0:4], refs[4:8], refs[8:12], refs[12]
    inward = [pltpu.make_async_copy(a, b, sems.at[0, i]) for i, (a, b) in enumerate(zip(sources, held))]
    outward = [pltpu.make_async_copy(a, b, sems.at[1, i]) for i, (a, b) in enumerate(zip(held, targets))]
    for copy in inward:
        copy.start()
    for first, second in zip(inward, outward):
        first.wait()
        second.start()
    for copy in outward:
        copy.wait()


def on_device(features, w_self, w_neigh, tiles, dest, outside, cotangent):
    hbm = pl.BlockSpec(memory_space=pltpu.HBM)
    dma = pltpu.SemaphoreType.DMA
    V = pltpu.VMEM
    results = pl.pallas_call(
        kernel,
        out_shape=(
            jax.ShapeDtypeStruct((B, B), BF),
            jax.ShapeDtypeStruct((B, B), BF),
            jax.ShapeDtypeStruct((2, NY, 16, B), F32),
            jax.ShapeDtypeStruct((2, NY, 16, B), F32),
        ),
        in_specs=[hbm] * 7,
        out_specs=(hbm,) * 4,
        scratch_shapes=[
            V((B, B), BF), V((B, B), BF), V((B, B), BF), V((1, B), jnp.int32), V((1, B), jnp.int32),
            V((B, B), BF), V((B, B), BF), V((B, B), BF),
            V((B + 1, B, B), BF),
            V((NZ, NY, B, NX * B), BF),
            V((B, B), BF),
            V((8, B), jnp.int32),
            pltpu.SMEM((8, B), jnp.int32),
            V((B, B), F32),
            V((NZ, NX, NY, 32, B), BF),
            V((NZ, NY, NX, 32, B), BF),
            V((NZ, 3, NY, 32, B), BF),
            V((NZ, 3, NX, 32, B), BF),
            V((NZ, NY, 32, B), BF),
            V((NZ, NX, 32, B), BF),
            V((NZ - 1, NY, 32, B), BF),
            V((NZ - 1, NX, 32, B), BF),
            V((NY, 32, B), BF),
            V((NX, 32, B), BF),
            V((16, 32, B), BF),
            V((NX, NZ, 8, B), F32),
            V((3, NZ, 8, B), F32),
            V((NZ, 8, B), F32),
            V((NZ - 1, 8, B), F32),
            V((8, B), F32),
            V((3, 8, B), F32),
            V((B, B), F32),
            V((64, B), F32),
            V((NZ, NX, NY, 32, B), BF),
            V((NZ, NY, NX, 32, B), BF),
            V((4, 64, B), F32),
            V((3, 64, B), F32),
            V((4, 16, B), F32),
            V((3, 16, B), F32),
            V((NZ, 16, B), F32),
            V((NX, NY, 16, B), F32),
            V((B, B), F32),
            V((B, B), F32),
            dma((8,)),
            dma((2,)), dma((NZ,)), dma((NZ,)),
            dma((2,)), dma((2,)),
            dma(()), dma(()),
            dma((3,)), dma((3,)),
            dma((2,)), dma((2,)),
            dma((2,)), dma((NZ,)),
            dma((2,)), dma((NZ,)), dma((NZ,)),
            dma((2,)), dma((NZ,)), dma((NZ,)),
            dma((5,)), dma((5,)),
            dma((4,)),
        ],
        compiler_params=pltpu.CompilerParams(
            collective_id=0, has_side_effects=True, vmem_limit_bytes=60 * 2**20
        ),
        name="sage",
    )(features, w_self, w_neigh, tiles, dest.reshape(1, B), outside.reshape(1, B), cotangent)
    results = pl.pallas_call(
        hand_out,
        out_shape=tuple(jax.ShapeDtypeStruct(r.shape, r.dtype) for r in results),
        in_specs=[hbm] * 4,
        out_specs=(hbm,) * 4,
        scratch_shapes=[V(r.shape, r.dtype) for r in results] + [dma((2, 4))],
        compiler_params=pltpu.CompilerParams(vmem_limit_bytes=60 * 2**20),
        name="hand_out",
    )(*results)
    output, grad_input, grad_self, grad_neigh = results
    return output, grad_input, grad_self.reshape(B, B), grad_neigh.reshape(B, B)


def solution(mesh):
    placed = (
        P("dom", None),
        P(None, "feat"),
        P(None, "feat"),
        P("dom", None, None),
        P("dom", None),
        P("dom"),
        P("dom", "feat"),
    )
    return jax.shard_map(
        on_device,
        mesh=mesh,
        in_specs=placed,
        out_specs=(P("dom", "feat"), P("dom", None), P(None, "feat"), P(None, "feat")),
        check_vma=False,
    )
```

```python
import jax
import jax.numpy as jnp
from jax import lax
from jax.experimental import pallas as pl
from jax.experimental.pallas import tpu as pltpu
from jax.sharding import PartitionSpec as P

MESH = pl.DeviceIdType.MESH
BF = jnp.bfloat16
F32 = jnp.float32
NX, NY, NZ = 4, 4, 8
B = 128
SPREAD = (2, 1, 3)
SLANTED = 0
PLAN = ('s1', 's2', 't0', 'w2', 's3', 's4', 't1', 't2', 's5', 's6', 't3', 'w3', 's7', 'l0', 't4', 'l1', 't5', 'w4', 'l2', 't6', 'l3', 't7', 'w5', 'l4', 'l5', 'l6', 'l7')


def far_first(p):
    half = (p + 1) // 2
    return 4 + half * (1 - 2 * (p % 2))


def kernel(
    feat_h, ws_h, wn_h, tiles_h, dest_h, outside_h, cot_h,
    out_h, gi_h, gs_h, gn_h,
    feat, ws, wn, dest, outside, cot, out_o, gi_o,
    tiles, adj, xt, idx_v, idx_s, selfp,
    sx, sy, r1x, r1y, p1x, p1y, r2x, r2y, rpx, rpy, p2x, p2y, r3,
    lk, rlk1, plk, rlk2, lk2, rlk3,
    gpart, grecv, gx, gy,
    w0, rw1, w1, rw2, rw3, wg, gis, gir,
    load_sem, s1, rs1x, rs1y, s2, rs2, rsp, s3, rs3, sl, rsl, sg, rsg,
    sa, ra, sb, rbx, rby, sc, rcx, rcy, sw, rw, out_sem, past,
):
    dom = lax.axis_index("dom")
    c = lax.axis_index("feat")
    x = lax.rem(dom, NX)
    z = lax.rem(dom // NX, NZ)
    y = dom // (NX * NZ)
    oc = 1 - c

    def dev(px, py, pz, pc):
        return ((py * NZ + pz) * NX + px, pc)

    def xp(k):
        return lax.rem(x + k, NX)

    def yp(k):
        return lax.rem(y + k, NY)

    def zp(k):
        return lax.rem(z + k, NZ)

    def push(src, dst, send, recv, device):
        pltpu.make_async_remote_copy(
            src_ref=src, dst_ref=dst, send_sem=send, recv_sem=recv,
            device_id=device, device_id_type=MESH,
        ).start()

    def take(ref, sem):
        pltpu.make_async_copy(ref, ref, sem).wait()

    debts = []

    def owe(ref, sem):
        debts.append((ref, sem))

    def settle():
        for ref, sem in debts:
            take(ref, sem)

    loads = [
        pltpu.make_async_copy(src, dst, load_sem.at[i])
        for i, (src, dst) in enumerate(
            (
                (dest_h, dest), (feat_h, feat), (ws_h, ws),
                (wn_h, wn), (cot_h, cot), (outside_h, outside),
            )
        )
    ]
    for i in range(4):
        part = pl.ds(i * 32, 32)
        loads.append(pltpu.make_async_copy(tiles_h.at[part], tiles.at[part], load_sem.at[7 + i]))
    for load in loads:
        load.start()

    barrier = pltpu.get_barrier_semaphore()
    line = [dev(xp(k), y, z, c) for k in (1, 2, 3)] + [dev(x, yp(k), z, c) for k in (1, 2, 3)]
    line += [dev(x, y, zp(k), c) for k in range(1, NZ)] + [dev(x, y, z, oc)]
    for d in line:
        pl.semaphore_signal(barrier, inc=1, device_id=d, device_id_type=MESH)

    loads[0].wait()
    named = jnp.broadcast_to(dest[...], (B, B)).T
    lanes = lax.broadcasted_iota(jnp.int32, (B, B), 1)
    rows = lax.broadcasted_iota(jnp.int32, (B, B), 0)
    hit = named == lanes
    last = jnp.max(jnp.where(hit, rows, -1), axis=0, keepdims=True)
    first = jnp.min(jnp.where(hit, rows, B), axis=0, keepdims=True)
    idx_v[0:1, :] = first
    idx_v[1:2, :] = jnp.where(last > first, last, B)
    table = pltpu.make_async_copy(idx_v, idx_s, load_sem.at[6])
    table.start()
    tiles[B] = jnp.zeros((B, B), BF)
    loads[1].wait()
    features = feat[...]
    xt[0:B, :] = features.astype(F32).T.astype(BF)
    xh = xt[pl.ds(pl.multiple_of(c * 64, 64), 64), :]
    left = jnp.concatenate([xh, jnp.ones((16, B), BF)], axis=0)
    loads[2].wait()
    selfp[...] = jnp.dot(features, ws[...], preferred_element_type=F32)
    table.wait()
    for load in loads[6:]:
        load.wait()
    pl.semaphore_wait(barrier, len(line))
    pl.semaphore_signal(past, inc=1, device_id=dev(x, y, z, oc), device_id_type=MESH)

    def first_phase(p):
        dz = zp(far_first(p))
        for py in range(NY):
            parts = []
            for px in range(NX):
                d = (py * NZ + dz) * NX + px
                both = tiles[idx_s[0, d]] + tiles[idx_s[1, d]]
                adj[p, py, :, px * B:(px + 1) * B] = both
                parts.append(both)
            o = jnp.dot(left, jnp.concatenate(parts, axis=1), preferred_element_type=F32)
            for px in range(NX):
                part = o[:, px * B:(px + 1) * B]
                sx[p, px, py] = part[0:32].astype(BF)
                sy[p, py, px] = part[32:64].astype(BF)
                lk[px + c * (py - px), p, pl.ds(py + c * (px - py), 1), :] = part[64:65]
        for k in SPREAD:
            push(sx.at[p, xp(k)], r1x.at[p, k - 1], s1.at[0], rs1x.at[p], dev(xp(k), y, z, c))
            push(sy.at[p, yp(k)], r1y.at[p, k - 1], s1.at[1], rs1y.at[p], dev(x, yp(k), z, c))

    def add_four(own, got):
        total = own.astype(F32)
        for k in range(3):
            total = total + got[k].astype(F32)
        return total

    joins = {3: 0, 4: 1}
    passed = {1: (1, 0), 2: (NZ - 1, 1)}
    slots = {0: 0, 3: 1, 4: 2, 5: 3, 6: 4}

    def second_phase(p):
        for share, own, got, sent, s_, r_, ready, passed_on, r_passed in (
            (0, sx.at[p, x], r1x, p1x, s2.at[0], r2x, rs1x, rpx, rsp),
            (1, sy.at[p, y], r1y, p1y, s2.at[1], r2y, rs1y, rpy, rsp),
        ):
            take(got.at[p], ready.at[p])
            total = add_four(own[...], got.at[p])
            if p in joins:
                take(passed_on.at[joins[p]], r_passed.at[share, joins[p]])
                total = total + passed_on[joins[p]].astype(F32)
            sent[p] = total.astype(BF)
            if p in passed:
                k, side = passed[p]
                push(sent.at[p], passed_on.at[side], s_, r_passed.at[share, side], dev(x, y, zp(k), c))
            else:
                push(sent.at[p], r_.at[slots[p]], s_, rs2.at[share], dev(x, y, zp(far_first(p)), c))

    def each_first(p, carry):
        first_phase(p)
        return carry

    lax.fori_loop(0, NZ, each_first, 0)
    for k in SPREAD:
        to = dev(x + oc * (xp(k) - x), y + c * (yp(k) - y), z, c)
        push(lk.at[xp(k) + c * (yp(k) - xp(k))], rlk1.at[k - 1], sl.at[0], rsl.at[0], to)
    for p in range(NZ - 1):
        second_phase(p)
    owe(sx.at[:, pl.ds(0, 3)], s1.at[0])
    owe(sy.at[:, pl.ds(0, 3)], s1.at[1])
    owe(lk.at[pl.ds(0, 3)], sl.at[0])
    owe(p1x.at[pl.ds(0, 7)], s2.at[0])
    owe(p1y.at[pl.ds(0, 7)], s2.at[1])
    owe(plk.at[pl.ds(0, 7)], sl.at[1])
    take(rlk1, rsl.at[0])
    plk[...] = lk[x + c * (y - x)] + rlk1[0] + rlk1[1] + rlk1[2]
    for p in range(NZ - 1):
        push(plk.at[p], rlk2.at[p], sl.at[1], rsl.at[1], dev(x, y, zp(far_first(p)), c))
    own = NZ - 1
    take(r1x.at[own], rs1x.at[own])
    keep_x = add_four(sx[own, x], r1x.at[own])
    take(r1y.at[own], rs1y.at[own])
    keep_y = add_four(sy[own, y], r1y.at[own])

    pl.semaphore_wait(past, 1)
    take(r2x, rs2.at[0])
    for i in range(5):
        keep_x = keep_x + r2x[i].astype(F32)
    p2x[...] = keep_x.astype(BF)
    for pc in (c, oc):
        for k in SPREAD:
            push(p2x.at[yp(k)], r3.at[c * 4 + k], s3, rs3, dev(x, yp(k), z, pc))
    push(p2x.at[y], r3.at[c * 4], s3, rs3, dev(x, y, z, oc))
    take(r2y, rs2.at[1])
    for i in range(5):
        keep_y = keep_y + r2y[i].astype(F32)
    p2y[...] = keep_y.astype(BF)
    for pc in (c, oc):
        for k in SPREAD:
            push(p2y.at[xp(k)], r3.at[8 + c * 4 + k], s3, rs3, dev(xp(k), y, z, pc))
    push(p2y.at[x], r3.at[8 + c * 4], s3, rs3, dev(x, y, z, oc))
    take(rlk2, rsl.at[1])
    total = plk[own]
    for p in range(NZ - 1):
        total = total + rlk2[p]
    lk2[...] = total
    for k in SPREAD:
        to = dev(x + c * (xp(k) - x), y + oc * (yp(k) - y), z, c)
        push(lk2, rlk3.at[k - 1], sl.at[2], rsl.at[2], to)
    r3[c * 4] = p2x[y]
    r3[8 + c * 4] = p2y[x]
    owe(r3.at[pl.ds(0, 14)], s3)
    owe(rlk3, sl.at[2])
    loads[5].wait()
    take(rlk3, rsl.at[2])
    row = pl.ds(y + c * (x - y), 1)
    links = lk2[row, :]
    for k in range(3):
        links = links + rlk3[k, row, :]
    inverse = 1.0 / (links + outside[...].astype(F32))
    take(r3.at[pl.ds(0, 14)], rs3)
    pieces = []
    for pc in range(2):
        for share in range(2):
            slot = share * 8 + pc * 4
            piece = r3[slot].astype(F32)
            for k in range(1, 4):
                piece = piece + r3[slot + k].astype(F32)
            pieces.append(piece)
    mean_t = jnp.concatenate(pieces, axis=0) * inverse
    mean_tb = mean_t.astype(BF)

    loads[3].wait()
    loads[4].wait()
    pre = selfp[...] + jnp.dot(mean_t.T.astype(BF), wn[...], preferred_element_type=F32)
    sigma = jax.nn.sigmoid(pre)
    out_o[...] = (pre * sigma).astype(BF)
    emit = [pltpu.make_async_copy(out_o, out_h, out_sem.at[0])]
    emit[0].start()
    dpre = (cot[...].astype(F32) * sigma * (1.0 + pre * (1.0 - sigma))).astype(BF)
    across = (((1,), (1,)), ((), ()))
    gpart[...] = lax.dot_general(wn[...], dpre, across, preferred_element_type=F32) * inverse
    push(gpart.at[pl.ds(pl.multiple_of(oc * 64, 64), 64)], grecv, sg.at[0], rsg.at[0], dev(x, y, z, oc))
    owe(grecv, sg.at[0])
    grad_s = jnp.dot(xt[...], dpre, preferred_element_type=F32)
    grad_n = jnp.dot(mean_tb, dpre, preferred_element_type=F32)
    w0[0] = grad_s.reshape(4, 32, B)
    w0[1] = grad_n.reshape(4, 32, B)
    for k in SPREAD:
        push(w0.at[0, xp(k)], rw1.at[k - 1], sw.at[0], rw.at[0], dev(xp(k), y, z, c))
        push(w0.at[1, yp(k)], rw1.at[k + 2], sw.at[0], rw.at[0], dev(x, yp(k), z, c))
    owe(rw1, sw.at[0])
    direct = lax.dot_general(dpre, ws[...], across, preferred_element_type=F32)
    take(grecv, rsg.at[0])
    gfull = (gpart[pl.ds(pl.multiple_of(c * 64, 64), 64), :] + grecv[...]).astype(BF)
    gx[0, x, y] = gfull[0:32]
    gy[0, y, x] = gfull[32:64]

    near = (0, 7, 1, 6, 2, 5, 3, 4)
    def along_second(q):
        there = zp(NZ - near[q])
        for k in SPREAD:
            push(gx.at[0, x, y], gx.at[q, x, y], sb.at[0], rbx.at[q], dev(x, yp(k), there, c))
            push(gy.at[0, y, x], gy.at[q, y, x], sb.at[1], rby.at[q], dev(xp(k), y, there, c))

    along_second(0)
    for q in range(1, NZ):
        to = dev(x, y, zp(NZ - near[q]), c)
        push(gx.at[0, x, y], gx.at[q, x, y], sa.at[0], ra.at[q], to)
        push(gy.at[0, y, x], gy.at[q, y, x], sa.at[1], ra.at[q], to)
        if q <= SLANTED:
            along_second(q)
    owe(gx.at[0, 0, pl.ds(0, 4)], sa.at[0])
    owe(gx.at[0, 0, pl.ds(0, 3)], sa.at[0])
    owe(gy.at[0, 0, pl.ds(0, 4)], sa.at[1])
    owe(gy.at[0, 0, pl.ds(0, 3)], sa.at[1])

    def across_second(q):
        take(gx.at[q, x, pl.ds(0, 2)], ra.at[q])
        for k in SPREAD:
            push(gx.at[q, x, y], gx.at[q, x, y], sb.at[0], rbx.at[q], dev(x, yp(k), z, c))
            push(gy.at[q, y, x], gy.at[q, y, x], sb.at[1], rby.at[q], dev(xp(k), y, z, c))

    def across_third(q):
        if 0 < q <= SLANTED:
            take(gx.at[q, x, pl.ds(0, 2)], ra.at[q])
        take(gx.at[q, x, pl.ds(0, 3)], rbx.at[q])
        for k in SPREAD:
            push(gx.at[q, x], gx.at[q, x], sc.at[0], rcx.at[q], dev(xp(k), y, z, c))
        take(gy.at[q, y, pl.ds(0, 3)], rby.at[q])
        for k in SPREAD:
            push(gy.at[q, y], gy.at[q, y], sc.at[1], rcy.at[q], dev(x, yp(k), z, c))

    def last_phase(q, acc):
        take(gx.at[q, pl.ds(0, 3)], rcx.at[q])
        take(gy.at[q, pl.ds(0, 3)], rcy.at[q])
        for py in range(NY):
            right = jnp.concatenate(
                [jnp.concatenate([gx[q, px, py], gy[q, py, px]], axis=0) for px in range(NX)], axis=1
            )
            acc = acc + lax.dot_general(adj[NZ - 1 - q, py], right, across, preferred_element_type=F32)
        return acc

    def weights_second():
        take(rw1, rw.at[0])
        for share, own in ((0, x), (1, y)):
            part = w0[share, own]
            for k in range(3):
                part = part + rw1[3 * share + k]
            w1[share] = part.reshape(4, 8, B)
        for k in SPREAD:
            push(w1.at[0, yp(k)], rw2.at[k - 1], sw.at[1], rw.at[1], dev(x, yp(k), z, c))
            push(w1.at[1, xp(k)], rw2.at[k + 2], sw.at[1], rw.at[1], dev(xp(k), y, z, c))
        owe(rw2, sw.at[1])

    def weights_third():
        take(rw2, rw.at[1])
        rw3[z, 0] = w1[0, y] + rw2[0] + rw2[1] + rw2[2]
        rw3[z, 1] = w1[1, x] + rw2[3] + rw2[4] + rw2[5]
        for k in range(1, NZ):
            push(rw3.at[z], rw3.at[z], sw.at[2], rw.at[2], dev(x, y, zp(k), c))
        owe(rw3.at[pl.ds(0, 7)], sw.at[2])

    def weights_fourth():
        take(rw3.at[pl.ds(0, 7)], rw.at[2])
        total = rw3[0]
        for k in range(1, NZ):
            total = total + rw3[k]
        wg[0, x, y] = total[0]
        wg[1, y, x] = total[1]
        for k in SPREAD:
            push(wg.at[0, x, y], wg.at[0, x, y], sw.at[3], rw.at[3], dev(x, yp(k), z, c))
            push(wg.at[1, y, x], wg.at[1, y, x], sw.at[3], rw.at[3], dev(xp(k), y, z, c))
        owe(rw2, sw.at[3])

    def weights_fifth():
        take(rw2, rw.at[3])
        for k in SPREAD:
            push(wg.at[0, x], wg.at[0, x], sw.at[4], rw.at[4], dev(xp(k), y, z, c))
            push(wg.at[1, y], wg.at[1, y], sw.at[4], rw.at[4], dev(x, yp(k), z, c))
        owe(rw1, sw.at[4])

    acc = jnp.zeros((B, 64), F32)
    weights = {2: weights_second, 3: weights_third, 4: weights_fourth, 5: weights_fifth}
    for step in PLAN:
        what, q = step[0], int(step[1])
        if what == "s":
            across_second(q)
        elif what == "t":
            across_third(q)
        elif what == "w":
            weights[q]()
        else:
            acc = last_phase(q, acc)
    owe(gx.at[:, 0, pl.ds(0, 3)], sb.at[0])
    owe(gy.at[:, 0, pl.ds(0, 3)], sb.at[1])
    owe(gx.at[:, pl.ds(0, 3)], sc.at[0])
    owe(gy.at[:, pl.ds(0, 3)], sc.at[1])

    none = jnp.zeros((B, 64), F32)
    placed = jnp.where(c == 0, jnp.concatenate([acc, none], axis=1), jnp.concatenate([none, acc], axis=1))
    gis[...] = placed + direct
    push(gis, gir, sg.at[1], rsg.at[1], dev(x, y, z, oc))
    take(rw1, rw.at[4])
    emit.append(pltpu.make_async_copy(wg.at[0], gs_h, out_sem.at[1]))
    emit.append(pltpu.make_async_copy(wg.at[1], gn_h, out_sem.at[2]))
    emit[1].start()
    emit[2].start()

    settle()
    take(gir, rsg.at[1])
    gi_o[...] = (gis[...] + gir[...]).astype(BF)
    emit.append(pltpu.make_async_copy(gi_o, gi_h, out_sem.at[3]))
    emit[3].start()
    take(gis, sg.at[1])
    for copy in emit:
        copy.wait()


def hand_out(*refs):
    sources, targets, held, sems = refs[0:4], refs[4:8], refs[8:12], refs[12]
    inward = [pltpu.make_async_copy(a, b, sems.at[0, i]) for i, (a, b) in enumerate(zip(sources, held))]
    outward = [pltpu.make_async_copy(a, b, sems.at[1, i]) for i, (a, b) in enumerate(zip(held, targets))]
    for copy in inward:
        copy.start()
    for first, second in zip(inward, outward):
        first.wait()
        second.start()
    for copy in outward:
        copy.wait()


def on_device(features, w_self, w_neigh, tiles, dest, outside, cotangent):
    hbm = pl.BlockSpec(memory_space=pltpu.HBM)
    dma = pltpu.SemaphoreType.DMA
    V = pltpu.VMEM
    results = pl.pallas_call(
        kernel,
        out_shape=(
            jax.ShapeDtypeStruct((B, B), BF),
            jax.ShapeDtypeStruct((B, B), BF),
            jax.ShapeDtypeStruct((4, 4, 8, B), F32),
            jax.ShapeDtypeStruct((4, 4, 8, B), F32),
        ),
        in_specs=[hbm] * 7,
        out_specs=(hbm,) * 4,
        scratch_shapes=[
            V((B, B), BF), V((B, B), BF), V((B, B), BF), V((1, B), jnp.int32), V((1, B), jnp.int32),
            V((B, B), BF), V((B, B), BF), V((B, B), BF),
            V((B + 1, B, B), BF),
            V((NZ, NY, B, NX * B), BF),
            V((B, B), BF),
            V((8, B), jnp.int32),
            pltpu.SMEM((8, B), jnp.int32),
            V((B, B), F32),
            V((NZ, NX, NY, 32, B), BF),
            V((NZ, NY, NX, 32, B), BF),
            V((NZ, 3, NY, 32, B), BF),
            V((NZ, 3, NX, 32, B), BF),
            V((NZ, NY, 32, B), BF),
            V((NZ, NX, 32, B), BF),
            V((5, NY, 32, B), BF),
            V((5, NX, 32, B), BF),
            V((2, NY, 32, B), BF),
            V((2, NX, 32, B), BF),
            V((NY, 32, B), BF),
            V((NX, 32, B), BF),
            V((16, 32, B), BF),
            V((NX, NZ, 4, B), F32),
            V((3, NZ, 4, B), F32),
            V((NZ, 4, B), F32),
            V((NZ - 1, 4, B), F32),
            V((4, B), F32),
            V((3, 4, B), F32),
            V((B, B), F32),
            V((64, B), F32),
            V((NZ, NX, NY, 32, B), BF),
            V((NZ, NY, NX, 32, B), BF),
            V((2, 4, 32, B), F32),
            V((6, 32, B), F32),
            V((2, 4, 8, B), F32),
            V((6, 8, B), F32),
            V((NZ, 2, 8, B), F32),
            V((2, 4, 4, 8, B), F32),
            V((B, B), F32),
            V((B, B), F32),
            dma((11,)),
            dma((2,)), dma((NZ,)), dma((NZ,)),
            dma((2,)), dma((2,)), dma((2, 2)),
            dma(()), dma(()),
            dma((3,)), dma((3,)),
            dma((2,)), dma((2,)),
            dma((2,)), dma((NZ,)),
            dma((2,)), dma((NZ,)), dma((NZ,)),
            dma((2,)), dma((NZ,)), dma((NZ,)),
            dma((5,)), dma((5,)),
            dma((4,)),
            pltpu.SemaphoreType.REGULAR,
        ],
        compiler_params=pltpu.CompilerParams(
            collective_id=0, has_side_effects=True, vmem_limit_bytes=60 * 2**20
        ),
        name="sage",
    )(features, w_self, w_neigh, tiles, dest.reshape(1, B), outside.reshape(1, B), cotangent)
    results = pl.pallas_call(
        hand_out,
        out_shape=tuple(jax.ShapeDtypeStruct(r.shape, r.dtype) for r in results),
        in_specs=[hbm] * 4,
        out_specs=(hbm,) * 4,
        scratch_shapes=[V(r.shape, r.dtype) for r in results] + [dma((2, 4))],
        compiler_params=pltpu.CompilerParams(vmem_limit_bytes=60 * 2**20),
        name="hand_out",
    )(*results)
    output, grad_input, grad_self, grad_neigh = results
    return output, grad_input, grad_self.reshape(B, B), grad_neigh.reshape(B, B)


def solution(mesh):
    placed = (
        P("dom", None),
        P(None, "feat"),
        P(None, "feat"),
        P("dom", None, None),
        P("dom", None),
        P("dom"),
        P("dom", "feat"),
    )
    return jax.shard_map(
        on_device,
        mesh=mesh,
        in_specs=placed,
        out_specs=(P("dom", "feat"), P("dom", None), P(None, "feat"), P(None, "feat")),
        check_vma=False,
    )
```

```python
import jax
import jax.numpy as jnp
from jax import lax
from jax.experimental import pallas as pl
from jax.experimental.pallas import tpu as pltpu
from jax.sharding import PartitionSpec as P

MESH = pl.DeviceIdType.MESH
BF = jnp.bfloat16
F32 = jnp.float32
NX, NY, NZ = 4, 4, 8
B = 128
SPREAD = (2, 1, 3)
PLAN = ('s3', 's4', 't0', 's5', 's6', 'w2', 's7', 't3', 't4', 'r0', 't5', 't6', 'l0', 'w3', 't7', 'l3', 'l4', 'l5', 'l6', 'l1', 'l2', 'l7')


STEPS = (1, 7, 3, 5, 4, 2, 6, 0)
OWN = 7
PACKED = sum(step * 8**i for i, step in enumerate(STEPS))


def kernel(
    feat_h, ws_h, wn_h, tiles_h, dest_h, outside_h, cot_h,
    out_h, gi_h, gs_h, gn_h,
    feat, ws, wn, dest, outside, cot, out_o, gi_o,
    tiles, adj, xt, idx_v, idx_s, selfp,
    sx, sy, r1x, r1y, p1x, p1y, r2x, r2y, rawx, rawy, rawl, rpx, rpy, p2x, p2y, r3,
    lk, rlk1, plk, rlk2, lk2, rlk3,
    gpart, grecv, gx, gy,
    w0, rw1, rw3, wg, gis, gir,
    load_sem, s1, rraw, rs1x, rs1y, s2, rs2, rsp, s3, rs3, sl, rsl, rsl1, sg, rsg,
    sa, ra, sb, rbx, rby, sc, rcx, rcy, sw, rw, out_sem, past,
):
    dom = lax.axis_index("dom")
    c = lax.axis_index("feat")
    x = lax.rem(dom, NX)
    z = lax.rem(dom // NX, NZ)
    y = dom // (NX * NZ)
    oc = 1 - c

    def dev(px, py, pz, pc):
        return ((py * NZ + pz) * NX + px, pc)

    def xp(k):
        return lax.rem(x + k, NX)

    def yp(k):
        return lax.rem(y + k, NY)

    def zp(k):
        return lax.rem(z + k, NZ)

    def push(src, dst, send, recv, device):
        pltpu.make_async_remote_copy(
            src_ref=src, dst_ref=dst, send_sem=send, recv_sem=recv,
            device_id=device, device_id_type=MESH,
        ).start()

    def take(ref, sem):
        pltpu.make_async_copy(ref, ref, sem).wait()

    debts = []

    def owe(ref, sem):
        debts.append((ref, sem))

    def settle():
        for ref, sem in debts:
            take(ref, sem)

    loads = [
        pltpu.make_async_copy(src, dst, load_sem.at[i])
        for i, (src, dst) in enumerate(
            (
                (dest_h, dest), (feat_h, feat), (ws_h, ws),
                (wn_h, wn), (cot_h, cot), (outside_h, outside),
            )
        )
    ]
    for i in range(4):
        part = pl.ds(i * 32, 32)
        loads.append(pltpu.make_async_copy(tiles_h.at[part], tiles.at[part], load_sem.at[7 + i]))
    for load in loads:
        load.start()

    barrier = pltpu.get_barrier_semaphore()
    line = [dev(xp(k), y, z, c) for k in (1, 2, 3)] + [dev(x, yp(k), z, c) for k in (1, 2, 3)]
    line += [dev(x, y, zp(k), c) for k in range(1, NZ)] + [dev(x, y, z, oc)]
    for d in line:
        pl.semaphore_signal(barrier, inc=1, device_id=d, device_id_type=MESH)

    loads[0].wait()
    named = jnp.broadcast_to(dest[...], (B, B)).T
    lanes = lax.broadcasted_iota(jnp.int32, (B, B), 1)
    rows = lax.broadcasted_iota(jnp.int32, (B, B), 0)
    hit = named == lanes
    last = jnp.max(jnp.where(hit, rows, -1), axis=0, keepdims=True)
    first = jnp.min(jnp.where(hit, rows, B), axis=0, keepdims=True)
    idx_v[0:1, :] = first
    idx_v[1:2, :] = jnp.where(last > first, last, B)
    table = pltpu.make_async_copy(idx_v, idx_s, load_sem.at[6])
    table.start()
    tiles[B] = jnp.zeros((B, B), BF)
    loads[1].wait()
    features = feat[...]
    xt[0:B, :] = features.astype(F32).T.astype(BF)
    xh = xt[pl.ds(pl.multiple_of(c * 64, 64), 64), :]
    left = jnp.concatenate([xh, jnp.ones((16, B), BF)], axis=0)
    loads[2].wait()
    selfp[...] = jnp.dot(features, ws[...], preferred_element_type=F32)
    table.wait()
    for load in loads[6:]:
        load.wait()
    pl.semaphore_wait(barrier, len(line))
    pl.semaphore_signal(past, inc=1, device_id=dev(x, y, z, oc), device_id_type=MESH)

    def partial_sums(p, dz):
        to_z = zp(dz)
        for py in range(NY):
            parts = []
            for px in range(NX):
                d = (py * NZ + to_z) * NX + px
                both = tiles[idx_s[0, d]] + tiles[idx_s[1, d]]
                adj[p, py, :, px * B:(px + 1) * B] = both
                parts.append(both)
            o = jnp.dot(left, jnp.concatenate(parts, axis=1), preferred_element_type=F32)
            for px in range(NX):
                part = o[:, px * B:(px + 1) * B]
                sx[p, px, py] = part[0:32].astype(BF)
                sy[p, py, px] = part[32:64].astype(BF)
                lk[p, px + c * (py - px), pl.ds(py + c * (px - py), 1), :] = part[64:65]

    def send_first(p):
        for k in SPREAD:
            push(sx.at[p, xp(k)], r1x.at[p, k - 1], s1.at[0], rs1x.at[p], dev(xp(k), y, z, c))
            push(sy.at[p, yp(k)], r1y.at[p, k - 1], s1.at[1], rs1y.at[p], dev(x, yp(k), z, c))
        for k in SPREAD:
            to = dev(x + oc * (xp(k) - x), y + c * (yp(k) - y), z, c)
            push(lk.at[p, xp(k) + c * (yp(k) - xp(k))], rlk1.at[p, k - 1], sl.at[0], rsl1.at[p], to)

    def to_next(p, code):
        dz = lax.rem(code, 8)
        partial_sums(p, dz)
        to = dev(x, y, zp(dz), c)
        push(sx.at[p], rawx.at[p], s1.at[2], rraw.at[0], to)
        push(sy.at[p], rawy.at[p], s1.at[3], rraw.at[1], to)
        push(lk.at[p], rawl.at[p], s1.at[4], rraw.at[2], to)
        return code // 8

    def to_far(p, code):
        partial_sums(p, lax.rem(code, 8))
        send_first(p)
        return code // 8

    lax.fori_loop(0, 2, to_next, PACKED)
    lax.fori_loop(2, OWN, to_far, PACKED // 64)
    partial_sums(OWN, 0)

    def send_own():
        for sent, raw, i in ((sx, rawx, 0), (sy, rawy, 1)):
            take(raw, rraw.at[i])
            for k in range(4):
                total = sent[OWN, k].astype(F32) + raw[0, k].astype(F32) + raw[1, k].astype(F32)
                sent[OWN, k] = total.astype(BF)
        take(rawl, rraw.at[2])
        lk[OWN] = lk[OWN] + rawl[0] + rawl[1]
        send_first(OWN)

    def add_four(own, got):
        total = own.astype(F32)
        for k in range(3):
            total = total + got[k].astype(F32)
        return total

    joins = {5: 0, 6: 1}
    passed = {2: (1, 0), 3: (NZ - 1, 1)}
    slots = {4: 0, 5: 1, 6: 2}

    def sum_links(p):
        take(rlk1.at[p], rsl1.at[p])
        plk[p] = lk[p, x + c * (y - x)] + rlk1[p, 0] + rlk1[p, 1] + rlk1[p, 2]

    def second_phase(p):
        for share, own, got, sent, s_, r_, ready, passed_on, r_passed in (
            (0, sx.at[p, x], r1x, p1x, s2.at[0], r2x, rs1x, rpx, rsp),
            (1, sy.at[p, y], r1y, p1y, s2.at[1], r2y, rs1y, rpy, rsp),
        ):
            take(got.at[p], ready.at[p])
            total = add_four(own[...], got.at[p])
            if p in joins:
                take(passed_on.at[joins[p]], r_passed.at[share, joins[p]])
                total = total + passed_on[joins[p]].astype(F32)
            sent[p] = total.astype(BF)
            if p in passed:
                k, side = passed[p]
                push(sent.at[p], passed_on.at[side], s_, r_passed.at[share, side], dev(x, y, zp(k), c))
            else:
                push(sent.at[p], r_.at[slots[p]], s_, rs2.at[share], dev(x, y, zp(STEPS[p]), c))

    for p in range(2, OWN):
        second_phase(p)
        sum_links(p)
        push(plk.at[p], rlk2.at[p - 2], sl.at[1], rsl.at[1], dev(x, y, zp(STEPS[p]), c))
        if p == 3:
            send_own()
    owe(sx.at[pl.ds(2, 6), pl.ds(0, 3)], s1.at[0])
    owe(sy.at[pl.ds(2, 6), pl.ds(0, 3)], s1.at[1])
    owe(rawx, s1.at[2])
    owe(rawy, s1.at[3])
    owe(rawl, s1.at[4])
    owe(lk.at[pl.ds(2, 6), pl.ds(0, 3)], sl.at[0])
    owe(p1x.at[pl.ds(0, 5)], s2.at[0])
    owe(p1y.at[pl.ds(0, 5)], s2.at[1])
    owe(plk.at[pl.ds(0, 5)], sl.at[1])
    own = OWN
    sum_links(own)
    take(r1x.at[own], rs1x.at[own])
    keep_x = add_four(sx[own, x], r1x.at[own])
    take(r1y.at[own], rs1y.at[own])
    keep_y = add_four(sy[own, y], r1y.at[own])

    pl.semaphore_wait(past, 1)
    take(r2x, rs2.at[0])
    for i in range(3):
        keep_x = keep_x + r2x[i].astype(F32)
    p2x[...] = keep_x.astype(BF)
    for pc in (c, oc):
        for k in SPREAD:
            push(p2x.at[yp(k)], r3.at[c * 4 + k], s3, rs3, dev(x, yp(k), z, pc))
    push(p2x.at[y], r3.at[c * 4], s3, rs3, dev(x, y, z, oc))
    take(r2y, rs2.at[1])
    for i in range(3):
        keep_y = keep_y + r2y[i].astype(F32)
    p2y[...] = keep_y.astype(BF)
    for pc in (c, oc):
        for k in SPREAD:
            push(p2y.at[xp(k)], r3.at[8 + c * 4 + k], s3, rs3, dev(xp(k), y, z, pc))
    push(p2y.at[x], r3.at[8 + c * 4], s3, rs3, dev(x, y, z, oc))
    take(rlk2, rsl.at[1])
    total = plk[own]
    for i in range(5):
        total = total + rlk2[i]
    lk2[...] = total
    for k in SPREAD:
        to = dev(x + c * (xp(k) - x), y + oc * (yp(k) - y), z, c)
        push(lk2, rlk3.at[k - 1], sl.at[2], rsl.at[2], to)
    r3[c * 4] = p2x[y]
    r3[8 + c * 4] = p2y[x]
    owe(r3.at[pl.ds(0, 14)], s3)
    owe(rlk3, sl.at[2])
    loads[5].wait()
    take(rlk3, rsl.at[2])
    row = pl.ds(y + c * (x - y), 1)
    links = lk2[row, :]
    for k in range(3):
        links = links + rlk3[k, row, :]
    inverse = 1.0 / (links + outside[...].astype(F32))
    take(r3.at[pl.ds(0, 14)], rs3)
    pieces = []
    for pc in range(2):
        for share in range(2):
            slot = share * 8 + pc * 4
            piece = r3[slot].astype(F32)
            for k in range(1, 4):
                piece = piece + r3[slot + k].astype(F32)
            pieces.append(piece)
    mean_t = jnp.concatenate(pieces, axis=0) * inverse
    mean_tb = mean_t.astype(BF)

    loads[3].wait()
    loads[4].wait()
    pre = selfp[...] + jnp.dot(mean_t.T.astype(BF), wn[...], preferred_element_type=F32)
    sigma = jax.nn.sigmoid(pre)
    out_o[...] = (pre * sigma).astype(BF)
    emit = [pltpu.make_async_copy(out_o, out_h, out_sem.at[0])]
    emit[0].start()
    dpre = (cot[...].astype(F32) * sigma * (1.0 + pre * (1.0 - sigma))).astype(BF)
    across = (((1,), (1,)), ((), ()))
    gpart[...] = lax.dot_general(wn[...], dpre, across, preferred_element_type=F32) * inverse
    push(gpart.at[pl.ds(pl.multiple_of(oc * 64, 64), 64)], grecv, sg.at[0], rsg.at[0], dev(x, y, z, oc))
    owe(grecv, sg.at[0])
    grad_s = jnp.dot(xt[...], dpre, preferred_element_type=F32)
    grad_n = jnp.dot(mean_tb, dpre, preferred_element_type=F32)
    w0[:, 0:8, :] = grad_s.reshape(16, 8, B)
    w0[:, 8:16, :] = grad_n.reshape(16, 8, B)
    here = x * NY + y
    plane = [(i, j) for i in (2, 1, 3, 0) for j in (2, 1, 3, 0) if (i, j) != (0, 0)]
    for i, j in plane:
        push(w0.at[xp(i) * NY + yp(j)], rw1.at[here], sw.at[0], rw.at[0], dev(xp(i), yp(j), z, c))
    owe(rw1.at[pl.ds(0, 15)], sw.at[0])
    direct = lax.dot_general(dpre, ws[...], across, preferred_element_type=F32)
    take(grecv, rsg.at[0])
    gfull = (gpart[pl.ds(pl.multiple_of(c * 64, 64), 64), :] + grecv[...]).astype(BF)
    gx[0, x, y] = gfull[0:32]
    gy[0, y, x] = gfull[32:64]

    near = (0, 7, 1, 6, 2, 5, 3, 4)
    for k in SPREAD:
        push(gx.at[0, x, y], gx.at[0, x, y], sb.at[0], rbx.at[0], dev(x, yp(k), z, c))
        push(gy.at[0, y, x], gy.at[0, y, x], sb.at[1], rby.at[0], dev(xp(k), y, z, c))
    for q in range(3, NZ):
        to = dev(x, y, zp(NZ - near[q]), c)
        push(gx.at[0, x, y], gx.at[q, x, y], sa.at[0], ra.at[q], to)
        push(gy.at[0, y, x], gy.at[q, y, x], sa.at[1], ra.at[q], to)
    owe(gx.at[pl.ds(0, 5), 0, 0], sa.at[0])
    owe(gy.at[pl.ds(0, 5), 0, 0], sa.at[1])

    def across_second(q):
        take(gx.at[q, x, pl.ds(0, 2)], ra.at[q])
        for k in SPREAD:
            push(gx.at[q, x, y], gx.at[q, x, y], sb.at[0], rbx.at[q], dev(x, yp(k), z, c))
            push(gy.at[q, y, x], gy.at[q, y, x], sb.at[1], rby.at[q], dev(xp(k), y, z, c))

    def across_third(q):
        take(gx.at[q, x, pl.ds(0, 3)], rbx.at[q])
        for k in SPREAD:
            push(gx.at[q, x], gx.at[q, x], sc.at[0], rcx.at[q], dev(xp(k), y, z, c))
        take(gy.at[q, y, pl.ds(0, 3)], rby.at[q])
        for k in SPREAD:
            push(gy.at[q, y], gy.at[q, y], sc.at[1], rcy.at[q], dev(x, yp(k), z, c))

    def plane_to_next():
        take(gx.at[0, pl.ds(0, 3)], rcx.at[0])
        take(gy.at[0, pl.ds(0, 3)], rcy.at[0])
        for q in (1, 2):
            to = dev(x, y, zp(NZ - near[q]), c)
            push(gx.at[0], gx.at[q], sc.at[2], rbx.at[q], to)
            push(gy.at[0], gy.at[q], sc.at[3], rby.at[q], to)

    def last_phase(q, acc):
        if q in (1, 2):
            take(gx.at[q], rbx.at[q])
            take(gy.at[q], rby.at[q])
        elif q > 2:
            take(gx.at[q, pl.ds(0, 3)], rcx.at[q])
            take(gy.at[q, pl.ds(0, 3)], rcy.at[q])
        for py in range(NY):
            right = jnp.concatenate(
                [jnp.concatenate([gx[q, px, py], gy[q, py, px]], axis=0) for px in range(NX)], axis=1
            )
            acc = acc + lax.dot_general(adj[STEPS.index(near[q]), py], right, across, preferred_element_type=F32)
        return acc

    def weights_second():
        rw1[here] = w0[here]
        take(rw1.at[pl.ds(0, 15)], rw.at[0])
        total = rw1[0]
        for k in range(1, 16):
            total = total + rw1[k]
        rw3[z] = total
        for k in range(1, NZ):
            push(rw3.at[z], rw3.at[z], sw.at[1], rw.at[1], dev(x, y, zp(k), c))
        owe(rw3.at[pl.ds(0, 7)], sw.at[1])

    def weights_third():
        take(rw3.at[pl.ds(0, 7)], rw.at[1])
        total = rw3[0]
        for k in range(1, NZ):
            total = total + rw3[k]
        wg[here] = total
        for i, j in plane:
            push(wg.at[here], wg.at[here], sw.at[2], rw.at[2], dev(xp(i), yp(j), z, c))
        owe(rw1.at[pl.ds(0, 15)], sw.at[2])

    acc = jnp.zeros((B, 64), F32)
    weights = {2: weights_second, 3: weights_third}
    for step in PLAN:
        what, q = step[0], int(step[1])
        if what == "s":
            across_second(q)
        elif what == "t":
            across_third(q)
        elif what == "w":
            weights[q]()
        elif what == "r":
            plane_to_next()
        else:
            acc = last_phase(q, acc)
    owe(gx.at[pl.ds(0, 6), 0, pl.ds(0, 3)], sb.at[0])
    owe(gy.at[pl.ds(0, 6), 0, pl.ds(0, 3)], sb.at[1])
    owe(gx.at[pl.ds(0, 6), pl.ds(0, 3)], sc.at[0])
    owe(gy.at[pl.ds(0, 6), pl.ds(0, 3)], sc.at[1])
    owe(gx.at[pl.ds(0, 2)], sc.at[2])
    owe(gy.at[pl.ds(0, 2)], sc.at[3])

    none = jnp.zeros((B, 64), F32)
    placed = jnp.where(c == 0, jnp.concatenate([acc, none], axis=1), jnp.concatenate([none, acc], axis=1))
    gis[...] = placed + direct
    push(gis, gir, sg.at[1], rsg.at[1], dev(x, y, z, oc))
    take(rw1.at[pl.ds(0, 15)], rw.at[2])
    emit.append(pltpu.make_async_copy(wg.at[:, pl.ds(0, 8)], gs_h, out_sem.at[1]))
    emit.append(pltpu.make_async_copy(wg.at[:, pl.ds(8, 8)], gn_h, out_sem.at[2]))
    emit[1].start()
    emit[2].start()

    settle()
    take(gir, rsg.at[1])
    gi_o[...] = (gis[...] + gir[...]).astype(BF)
    emit.append(pltpu.make_async_copy(gi_o, gi_h, out_sem.at[3]))
    emit[3].start()
    take(gis, sg.at[1])
    for copy in emit:
        copy.wait()


def hand_out(*refs):
    sources, targets, held, sems = refs[0:4], refs[4:8], refs[8:12], refs[12]
    inward = [pltpu.make_async_copy(a, b, sems.at[0, i]) for i, (a, b) in enumerate(zip(sources, held))]
    outward = [pltpu.make_async_copy(a, b, sems.at[1, i]) for i, (a, b) in enumerate(zip(held, targets))]
    for copy in inward:
        copy.start()
    for first, second in zip(inward, outward):
        first.wait()
        second.start()
    for copy in outward:
        copy.wait()


def on_device(features, w_self, w_neigh, tiles, dest, outside, cotangent):
    hbm = pl.BlockSpec(memory_space=pltpu.HBM)
    dma = pltpu.SemaphoreType.DMA
    V = pltpu.VMEM
    results = pl.pallas_call(
        kernel,
        out_shape=(
            jax.ShapeDtypeStruct((B, B), BF),
            jax.ShapeDtypeStruct((B, B), BF),
            jax.ShapeDtypeStruct((16, 8, B), F32),
            jax.ShapeDtypeStruct((16, 8, B), F32),
        ),
        in_specs=[hbm] * 7,
        out_specs=(hbm,) * 4,
        scratch_shapes=[
            V((B, B), BF), V((B, B), BF), V((B, B), BF), V((1, B), jnp.int32), V((1, B), jnp.int32),
            V((B, B), BF), V((B, B), BF), V((B, B), BF),
            V((B + 1, B, B), BF),
            V((NZ, NY, B, NX * B), BF),
            V((B, B), BF),
            V((8, B), jnp.int32),
            pltpu.SMEM((8, B), jnp.int32),
            V((B, B), F32),
            V((NZ, NX, NY, 32, B), BF),
            V((NZ, NY, NX, 32, B), BF),
            V((NZ, 3, NY, 32, B), BF),
            V((NZ, 3, NX, 32, B), BF),
            V((NZ, NY, 32, B), BF),
            V((NZ, NX, 32, B), BF),
            V((3, NY, 32, B), BF),
            V((3, NX, 32, B), BF),
            V((2, NX, NY, 32, B), BF),
            V((2, NY, NX, 32, B), BF),
            V((2, NX, 4, B), F32),
            V((2, NY, 32, B), BF),
            V((2, NX, 32, B), BF),
            V((NY, 32, B), BF),
            V((NX, 32, B), BF),
            V((16, 32, B), BF),
            V((NZ, NX, 4, B), F32),
            V((NZ, 3, 4, B), F32),
            V((NZ, 4, B), F32),
            V((5, 4, B), F32),
            V((4, B), F32),
            V((3, 4, B), F32),
            V((B, B), F32),
            V((64, B), F32),
            V((NZ, NX, NY, 32, B), BF),
            V((NZ, NY, NX, 32, B), BF),
            V((16, 16, B), F32),
            V((16, 16, B), F32),
            V((NZ, 16, B), F32),
            V((16, 16, B), F32),
            V((B, B), F32),
            V((B, B), F32),
            dma((11,)),
            dma((5,)), dma((3,)), dma((NZ,)), dma((NZ,)),
            dma((2,)), dma((2,)), dma((2, 2)),
            dma(()), dma(()),
            dma((3,)), dma((3,)), dma((NZ,)),
            dma((2,)), dma((2,)),
            dma((2,)), dma((NZ,)),
            dma((2,)), dma((NZ,)), dma((NZ,)),
            dma((4,)), dma((NZ,)), dma((NZ,)),
            dma((3,)), dma((3,)),
            dma((4,)),
            pltpu.SemaphoreType.REGULAR,
        ],
        compiler_params=pltpu.CompilerParams(
            collective_id=0, has_side_effects=True, vmem_limit_bytes=60 * 2**20
        ),
        name="sage",
    )(features, w_self, w_neigh, tiles, dest.reshape(1, B), outside.reshape(1, B), cotangent)
    results = pl.pallas_call(
        hand_out,
        out_shape=tuple(jax.ShapeDtypeStruct(r.shape, r.dtype) for r in results),
        in_specs=[hbm] * 4,
        out_specs=(hbm,) * 4,
        scratch_shapes=[V(r.shape, r.dtype) for r in results] + [dma((2, 4))],
        compiler_params=pltpu.CompilerParams(vmem_limit_bytes=60 * 2**20),
        name="hand_out",
    )(*results)
    output, grad_input, grad_self, grad_neigh = results
    return output, grad_input, grad_self.reshape(B, B), grad_neigh.reshape(B, B)


def solution(mesh):
    placed = (
        P("dom", None),
        P(None, "feat"),
        P(None, "feat"),
        P("dom", None, None),
        P("dom", None),
        P("dom"),
        P("dom", "feat"),
    )
    return jax.shard_map(
        on_device,
        mesh=mesh,
        in_specs=placed,
        out_specs=(P("dom", "feat"), P("dom", None), P(None, "feat"), P(None, "feat")),
        check_vma=False,
    )
```

```python
import jax
import jax.numpy as jnp
from jax import lax
from jax.experimental import pallas as pl
from jax.experimental.pallas import tpu as pltpu
from jax.sharding import PartitionSpec as P

MESH = pl.DeviceIdType.MESH
BF = jnp.bfloat16
F32 = jnp.float32
NX, NY, NZ = 4, 4, 8
B = 128
SPREAD = (2, 1, 3)
PLAN = ('s3', 's4', 't0', 's5', 's6', 'w2', 's7', 't3', 't4', 'r0', 't5', 't6', 't7', 'l0', 'w3', 'l3', 'l4', 'l5', 'l6', 'l1', 'l2', 'l7')


STEPS = (1, 7, 3, 5, 4, 2, 6, 0)
OWN = 7
PACKED = sum(step * 8**i for i, step in enumerate(STEPS))


def kernel(
    feat_h, ws_h, wn_h, tiles_h, dest_h, outside_h, cot_h,
    out_h, gis_h, gir_h, gs_h, gn_h,
    feat, ws, wn, dest, outside, cot, out_o,
    tiles, adj, xt, idx_v, idx_s, selfp, wnt, cott,
    sx, sy, r1x, r1y, p1x, p1y, r2x, r2y, rawx, rawy, rawl, rpx, rpy, p2x, p2y, r3,
    lk, rlk1, plk, rlk2, lk2, rlk3,
    gpart, grecv, gx, gy,
    w0, rw1, rw3, wg, gis,
    load_sem, s1, rraw, rs1x, rs1y, s2, rs2, rsp, s3, rs3, sl, rsl, rsl1, sg, rsg,
    sa, ra, sb, rbx, rby, sc, rcx, rcy, sw, rw, out_sem, past,
):
    dom = lax.axis_index("dom")
    c = lax.axis_index("feat")
    x = lax.rem(dom, NX)
    z = lax.rem(dom // NX, NZ)
    y = dom // (NX * NZ)
    oc = 1 - c

    def dev(px, py, pz, pc):
        return ((py * NZ + pz) * NX + px, pc)

    def xp(k):
        return lax.rem(x + k, NX)

    def yp(k):
        return lax.rem(y + k, NY)

    def zp(k):
        return lax.rem(z + k, NZ)

    def push(src, dst, send, recv, device):
        pltpu.make_async_remote_copy(
            src_ref=src, dst_ref=dst, send_sem=send, recv_sem=recv,
            device_id=device, device_id_type=MESH,
        ).start()

    def take(ref, sem):
        pltpu.make_async_copy(ref, ref, sem).wait()

    debts = []

    def owe(ref, sem):
        debts.append((ref, sem))

    def settle():
        for ref, sem in debts:
            take(ref, sem)

    loads = [
        pltpu.make_async_copy(src, dst, load_sem.at[i])
        for i, (src, dst) in enumerate(
            (
                (dest_h, dest), (feat_h, feat), (ws_h, ws),
                (wn_h, wn), (cot_h, cot), (outside_h, outside),
            )
        )
    ]
    for i in range(4):
        part = pl.ds(i * 32, 32)
        loads.append(pltpu.make_async_copy(tiles_h.at[part], tiles.at[part], load_sem.at[7 + i]))
    for load in loads:
        load.start()

    barrier = pltpu.get_barrier_semaphore()
    line = [dev(xp(k), y, z, c) for k in (1, 2, 3)] + [dev(x, yp(k), z, c) for k in (1, 2, 3)]
    line += [dev(x, y, zp(k), c) for k in range(1, NZ)] + [dev(x, y, z, oc)]
    for d in line:
        pl.semaphore_signal(barrier, inc=1, device_id=d, device_id_type=MESH)

    loads[0].wait()
    named = jnp.broadcast_to(dest[...], (B, B)).T
    lanes = lax.broadcasted_iota(jnp.int32, (B, B), 1)
    rows = lax.broadcasted_iota(jnp.int32, (B, B), 0)
    hit = named == lanes
    last = jnp.max(jnp.where(hit, rows, -1), axis=0, keepdims=True)
    first = jnp.min(jnp.where(hit, rows, B), axis=0, keepdims=True)
    idx_v[0:1, :] = first
    idx_v[1:2, :] = jnp.where(last > first, last, B)
    table = pltpu.make_async_copy(idx_v, idx_s, load_sem.at[6])
    table.start()
    tiles[B] = jnp.zeros((B, B), BF)
    loads[1].wait()
    features = feat[...]
    xt[0:B, :] = features.astype(F32).T.astype(BF)
    xh = xt[pl.ds(pl.multiple_of(c * 64, 64), 64), :]
    left = jnp.concatenate([xh, jnp.ones((16, B), BF)], axis=0)
    table.wait()
    for load in loads[6:]:
        load.wait()
    pl.semaphore_wait(barrier, len(line))
    pl.semaphore_signal(past, inc=1, device_id=dev(x, y, z, oc), device_id_type=MESH)

    def partial_sums(p, dz):
        to_z = zp(dz)
        for py in range(NY):
            parts = []
            for px in range(NX):
                d = (py * NZ + to_z) * NX + px
                both = tiles[idx_s[0, d]] + tiles[idx_s[1, d]]
                adj[p, py, :, px * B:(px + 1) * B] = both
                parts.append(both)
            o = jnp.dot(left, jnp.concatenate(parts, axis=1), preferred_element_type=F32)
            for px in range(NX):
                part = o[:, px * B:(px + 1) * B]
                sx[p, px, py] = part[0:32].astype(BF)
                sy[p, py, px] = part[32:64].astype(BF)
                lk[p, px + c * (py - px), pl.ds(py + c * (px - py), 1), :] = part[64:65]

    def send_first(p):
        for k in SPREAD:
            push(sx.at[p, xp(k)], r1x.at[p, k - 1], s1.at[0], rs1x.at[p], dev(xp(k), y, z, c))
            push(sy.at[p, yp(k)], r1y.at[p, k - 1], s1.at[1], rs1y.at[p], dev(x, yp(k), z, c))
        for k in SPREAD:
            to = dev(x + oc * (xp(k) - x), y + c * (yp(k) - y), z, c)
            push(lk.at[p, xp(k) + c * (yp(k) - xp(k))], rlk1.at[p, k - 1], sl.at[0], rsl1.at[p], to)

    def to_next(p, code):
        dz = code % 8
        partial_sums(p, dz)
        to = dev(x, y, zp(dz), c)
        push(sx.at[p], rawx.at[p], s1.at[2], rraw.at[0], to)
        push(sy.at[p], rawy.at[p], s1.at[3], rraw.at[1], to)
        push(lk.at[p], rawl.at[p], s1.at[4], rraw.at[2], to)
        return code // 8

    def to_far(p, code):
        partial_sums(p, code % 8)
        send_first(p)
        return code // 8

    to_far(2, PACKED // 64)
    lax.fori_loop(0, 2, to_next, PACKED)
    lax.fori_loop(3, OWN, to_far, PACKED // 512)
    partial_sums(OWN, 0)

    for load in loads[2:5]:
        load.wait()
    wnt[...] = wn[...].astype(F32).T.astype(BF)
    cott[...] = cot[...].astype(F32).T
    selfp[...] = jnp.dot(ws[...].astype(F32).T.astype(BF), xt[...], preferred_element_type=F32)

    def send_own():
        for sent, raw, i in ((sx, rawx, 0), (sy, rawy, 1)):
            take(raw, rraw.at[i])
            for k in range(4):
                total = sent[OWN, k].astype(F32) + raw[0, k].astype(F32) + raw[1, k].astype(F32)
                sent[OWN, k] = total.astype(BF)
        take(rawl, rraw.at[2])
        lk[OWN] = lk[OWN] + rawl[0] + rawl[1]
        send_first(OWN)

    def add_four(own, got):
        total = own.astype(F32)
        for k in range(3):
            total = total + got[k].astype(F32)
        return total

    joins = {5: 0, 6: 1}
    passed = {2: (1, 0), 3: (NZ - 1, 1)}
    slots = {4: 0, 5: 1, 6: 2}

    def sum_links(p):
        take(rlk1.at[p], rsl1.at[p])
        plk[p] = lk[p, x + c * (y - x)] + rlk1[p, 0] + rlk1[p, 1] + rlk1[p, 2]

    def second_phase(p):
        for share, own, got, sent, s_, r_, ready, passed_on, r_passed in (
            (0, sx.at[p, x], r1x, p1x, s2.at[0], r2x, rs1x, rpx, rsp),
            (1, sy.at[p, y], r1y, p1y, s2.at[1], r2y, rs1y, rpy, rsp),
        ):
            take(got.at[p], ready.at[p])
            total = add_four(own[...], got.at[p])
            if p in joins:
                take(passed_on.at[joins[p]], r_passed.at[share, joins[p]])
                total = total + passed_on[joins[p]].astype(F32)
            sent[p] = total.astype(BF)
            if p in passed:
                k, side = passed[p]
                push(sent.at[p], passed_on.at[side], s_, r_passed.at[share, side], dev(x, y, zp(k), c))
            else:
                push(sent.at[p], r_.at[slots[p]], s_, rs2.at[share], dev(x, y, zp(STEPS[p]), c))

    for p in range(2, OWN):
        second_phase(p)
        sum_links(p)
        push(plk.at[p], rlk2.at[p - 2], sl.at[1], rsl.at[1], dev(x, y, zp(STEPS[p]), c))
        if p == 3:
            send_own()
    owe(sx.at[pl.ds(2, 6), pl.ds(0, 3)], s1.at[0])
    owe(sy.at[pl.ds(2, 6), pl.ds(0, 3)], s1.at[1])
    owe(rawx, s1.at[2])
    owe(rawy, s1.at[3])
    owe(rawl, s1.at[4])
    owe(lk.at[pl.ds(2, 6), pl.ds(0, 3)], sl.at[0])
    owe(p1x.at[pl.ds(0, 5)], s2.at[0])
    owe(p1y.at[pl.ds(0, 5)], s2.at[1])
    owe(plk.at[pl.ds(0, 5)], sl.at[1])
    own = OWN
    sum_links(own)
    take(r1x.at[own], rs1x.at[own])
    keep_x = add_four(sx[own, x], r1x.at[own])
    take(r1y.at[own], rs1y.at[own])
    keep_y = add_four(sy[own, y], r1y.at[own])

    pl.semaphore_wait(past, 1)
    take(r2x, rs2.at[0])
    for i in range(3):
        keep_x = keep_x + r2x[i].astype(F32)
    p2x[...] = keep_x.astype(BF)
    for pc in (c, oc):
        for k in SPREAD:
            push(p2x.at[yp(k)], r3.at[c * 4 + k], s3, rs3, dev(x, yp(k), z, pc))
    push(p2x.at[y], r3.at[c * 4], s3, rs3, dev(x, y, z, oc))
    take(r2y, rs2.at[1])
    for i in range(3):
        keep_y = keep_y + r2y[i].astype(F32)
    p2y[...] = keep_y.astype(BF)
    for pc in (c, oc):
        for k in SPREAD:
            push(p2y.at[xp(k)], r3.at[8 + c * 4 + k], s3, rs3, dev(xp(k), y, z, pc))
    push(p2y.at[x], r3.at[8 + c * 4], s3, rs3, dev(x, y, z, oc))
    take(rlk2, rsl.at[1])
    total = plk[own]
    for i in range(5):
        total = total + rlk2[i]
    lk2[...] = total
    for k in SPREAD:
        to = dev(x + c * (xp(k) - x), y + oc * (yp(k) - y), z, c)
        push(lk2, rlk3.at[k - 1], sl.at[2], rsl.at[2], to)
    r3[c * 4] = p2x[y]
    r3[8 + c * 4] = p2y[x]
    owe(r3.at[pl.ds(0, 14)], s3)
    owe(rlk3, sl.at[2])
    loads[5].wait()
    take(rlk3, rsl.at[2])
    row = pl.ds(y + c * (x - y), 1)
    links = lk2[row, :]
    for k in range(3):
        links = links + rlk3[k, row, :]
    inverse = 1.0 / (links + outside[...].astype(F32))
    take(r3.at[pl.ds(0, 14)], rs3)
    pieces = []
    for pc in range(2):
        for share in range(2):
            slot = share * 8 + pc * 4
            piece = r3[slot].astype(F32)
            for k in range(1, 4):
                piece = piece + r3[slot + k].astype(F32)
            pieces.append(piece)
    mean_t = jnp.concatenate(pieces, axis=0) * inverse
    mean_tb = mean_t.astype(BF)

    pre = selfp[...] + jnp.dot(wnt[...], mean_tb, preferred_element_type=F32)
    sigma = jax.nn.sigmoid(pre)
    dpre_t = (cott[...] * sigma * (1.0 + pre * (1.0 - sigma))).astype(BF)
    across = (((1,), (1,)), ((), ()))
    gpart[...] = jnp.dot(wn[...], dpre_t, preferred_element_type=F32) * inverse
    push(gpart.at[pl.ds(pl.multiple_of(oc * 64, 64), 64)], grecv, sg.at[0], rsg.at[0], dev(x, y, z, oc))
    owe(grecv, sg.at[0])
    dpre = dpre_t.astype(F32).T.astype(BF)
    grad_s = jnp.dot(xt[...], dpre, preferred_element_type=F32)
    grad_n = jnp.dot(mean_tb, dpre, preferred_element_type=F32)
    w0[:, 0:8, :] = grad_s.reshape(16, 8, B)
    w0[:, 8:16, :] = grad_n.reshape(16, 8, B)
    here = x * NY + y
    plane = [(i, j) for i in (2, 1, 3, 0) for j in (2, 1, 3, 0) if (i, j) != (0, 0)]
    for i, j in plane:
        push(w0.at[xp(i) * NY + yp(j)], rw1.at[here], sw.at[0], rw.at[0], dev(xp(i), yp(j), z, c))
    owe(rw1.at[pl.ds(0, 15)], sw.at[0])
    direct = lax.dot_general(dpre, ws[...], across, preferred_element_type=F32)
    out_o[...] = (pre * sigma).T.astype(BF)
    emit = [pltpu.make_async_copy(out_o, out_h, out_sem.at[0])]
    emit[0].start()
    take(grecv, rsg.at[0])
    gfull = (gpart[pl.ds(pl.multiple_of(c * 64, 64), 64), :] + grecv[...]).astype(BF)
    gx[0, x, y] = gfull[0:32]
    gy[0, y, x] = gfull[32:64]

    near = (0, 7, 1, 6, 2, 5, 3, 4)
    for k in SPREAD:
        push(gx.at[0, x, y], gx.at[0, x, y], sb.at[0], rbx.at[0], dev(x, yp(k), z, c))
        push(gy.at[0, y, x], gy.at[0, y, x], sb.at[1], rby.at[0], dev(xp(k), y, z, c))
    for q in range(3, NZ):
        to = dev(x, y, zp(NZ - near[q]), c)
        push(gx.at[0, x, y], gx.at[q, x, y], sa.at[0], ra.at[q], to)
        push(gy.at[0, y, x], gy.at[q, y, x], sa.at[1], ra.at[q], to)
    owe(gx.at[pl.ds(0, 5), 0, 0], sa.at[0])
    owe(gy.at[pl.ds(0, 5), 0, 0], sa.at[1])

    def across_second(q):
        take(gx.at[q, x, pl.ds(0, 2)], ra.at[q])
        for k in SPREAD:
            push(gx.at[q, x, y], gx.at[q, x, y], sb.at[0], rbx.at[q], dev(x, yp(k), z, c))
            push(gy.at[q, y, x], gy.at[q, y, x], sb.at[1], rby.at[q], dev(xp(k), y, z, c))

    def across_third(q):
        take(gx.at[q, x, pl.ds(0, 3)], rbx.at[q])
        for k in SPREAD:
            push(gx.at[q, x], gx.at[q, x], sc.at[0], rcx.at[q], dev(xp(k), y, z, c))
        take(gy.at[q, y, pl.ds(0, 3)], rby.at[q])
        for k in SPREAD:
            push(gy.at[q, y], gy.at[q, y], sc.at[1], rcy.at[q], dev(x, yp(k), z, c))

    def plane_to_next():
        take(gx.at[0, pl.ds(0, 3)], rcx.at[0])
        take(gy.at[0, pl.ds(0, 3)], rcy.at[0])
        for q in (1, 2):
            to = dev(x, y, zp(NZ - near[q]), c)
            push(gx.at[0], gx.at[q], sc.at[2], rbx.at[q], to)
            push(gy.at[0], gy.at[q], sc.at[3], rby.at[q], to)

    def last_phase(q, acc):
        if q in (1, 2):
            take(gx.at[q], rbx.at[q])
            take(gy.at[q], rby.at[q])
        elif q > 2:
            take(gx.at[q, pl.ds(0, 3)], rcx.at[q])
            take(gy.at[q, pl.ds(0, 3)], rcy.at[q])
        for py in range(NY):
            right = jnp.concatenate(
                [jnp.concatenate([gx[q, px, py], gy[q, py, px]], axis=0) for px in range(NX)], axis=1
            )
            acc = acc + lax.dot_general(adj[STEPS.index(near[q]), py], right, across, preferred_element_type=F32)
        return acc

    def weights_second():
        rw1[here] = w0[here]
        take(rw1.at[pl.ds(0, 15)], rw.at[0])
        total = rw1[0]
        for k in range(1, 16):
            total = total + rw1[k]
        rw3[z] = total
        for k in range(1, NZ):
            push(rw3.at[z], rw3.at[z], sw.at[1], rw.at[1], dev(x, y, zp(k), c))
        owe(rw3.at[pl.ds(0, 7)], sw.at[1])

    def weights_third():
        take(rw3.at[pl.ds(0, 7)], rw.at[1])
        total = rw3[0]
        for k in range(1, NZ):
            total = total + rw3[k]
        wg[here] = total
        for i, j in plane:
            push(wg.at[here], wg.at[here], sw.at[2], rw.at[2], dev(xp(i), yp(j), z, c))
        owe(rw1.at[pl.ds(0, 15)], sw.at[2])

    acc = jnp.zeros((B, 64), F32)
    weights = {2: weights_second, 3: weights_third}
    for step in PLAN:
        what, q = step[0], int(step[1])
        if what == "s":
            across_second(q)
        elif what == "t":
            across_third(q)
        elif what == "w":
            weights[q]()
        elif what == "r":
            plane_to_next()
        else:
            acc = last_phase(q, acc)
    owe(gx.at[pl.ds(0, 6), 0, pl.ds(0, 3)], sb.at[0])
    owe(gy.at[pl.ds(0, 6), 0, pl.ds(0, 3)], sb.at[1])
    owe(gx.at[pl.ds(0, 6), pl.ds(0, 3)], sc.at[0])
    owe(gy.at[pl.ds(0, 6), pl.ds(0, 3)], sc.at[1])
    owe(gx.at[pl.ds(0, 2)], sc.at[2])
    owe(gy.at[pl.ds(0, 2)], sc.at[3])

    none = jnp.zeros((B, 64), F32)
    placed = jnp.where(c == 0, jnp.concatenate([acc, none], axis=1), jnp.concatenate([none, acc], axis=1))
    gis[...] = placed + direct
    push(gis, gir_h, sg.at[1], rsg.at[1], dev(x, y, z, oc))
    emit.append(pltpu.make_async_copy(gis, gis_h, out_sem.at[3]))
    emit[1].start()
    take(rw1.at[pl.ds(0, 15)], rw.at[2])
    emit.append(pltpu.make_async_copy(wg.at[:, pl.ds(0, 8)], gs_h, out_sem.at[1]))
    emit.append(pltpu.make_async_copy(wg.at[:, pl.ds(8, 8)], gn_h, out_sem.at[2]))
    emit[2].start()
    emit[3].start()

    settle()
    take(gis, rsg.at[1])
    take(gis, sg.at[1])
    for copy in emit:
        copy.wait()


def hand_out(out_h, gis_h, gir_h, gs_h, gn_h, out_t, gi_t, gs_t, gn_t, out, gis, gir, gs, gn, gi, sems):
    inward = [
        pltpu.make_async_copy(a, b, sems.at[0, i])
        for i, (a, b) in enumerate(((gis_h, gis), (gir_h, gir), (out_h, out), (gs_h, gs), (gn_h, gn)))
    ]
    outward = [
        pltpu.make_async_copy(a, b, sems.at[1, i])
        for i, (a, b) in enumerate(((gi, gi_t), (out, out_t), (gs, gs_t), (gn, gn_t)))
    ]
    for copy in inward:
        copy.start()
    inward[0].wait()
    inward[1].wait()
    gi[...] = (gis[...] + gir[...]).astype(BF)
    outward[0].start()
    for first, second in zip(inward[2:], outward[1:]):
        first.wait()
        second.start()
    for copy in outward:
        copy.wait()


def on_device(features, w_self, w_neigh, tiles, dest, outside, cotangent):
    hbm = pl.BlockSpec(memory_space=pltpu.HBM)
    dma = pltpu.SemaphoreType.DMA
    V = pltpu.VMEM
    results = pl.pallas_call(
        kernel,
        out_shape=(
            jax.ShapeDtypeStruct((B, B), BF),
            jax.ShapeDtypeStruct((B, B), F32),
            jax.ShapeDtypeStruct((B, B), F32),
            jax.ShapeDtypeStruct((16, 8, B), F32),
            jax.ShapeDtypeStruct((16, 8, B), F32),
        ),
        in_specs=[hbm] * 7,
        out_specs=(hbm,) * 5,
        scratch_shapes=[
            V((B, B), BF), V((B, B), BF), V((B, B), BF), V((1, B), jnp.int32), V((1, B), jnp.int32),
            V((B, B), BF), V((B, B), BF),
            V((B + 1, B, B), BF),
            V((NZ, NY, B, NX * B), BF),
            V((B, B), BF),
            V((8, B), jnp.int32),
            pltpu.SMEM((8, B), jnp.int32),
            V((B, B), F32),
            V((B, B), BF),
            V((B, B), F32),
            V((NZ, NX, NY, 32, B), BF),
            V((NZ, NY, NX, 32, B), BF),
            V((NZ, 3, NY, 32, B), BF),
            V((NZ, 3, NX, 32, B), BF),
            V((NZ, NY, 32, B), BF),
            V((NZ, NX, 32, B), BF),
            V((3, NY, 32, B), BF),
            V((3, NX, 32, B), BF),
            V((2, NX, NY, 32, B), BF),
            V((2, NY, NX, 32, B), BF),
            V((2, NX, 4, B), F32),
            V((2, NY, 32, B), BF),
            V((2, NX, 32, B), BF),
            V((NY, 32, B), BF),
            V((NX, 32, B), BF),
            V((16, 32, B), BF),
            V((NZ, NX, 4, B), F32),
            V((NZ, 3, 4, B), F32),
            V((NZ, 4, B), F32),
            V((5, 4, B), F32),
            V((4, B), F32),
            V((3, 4, B), F32),
            V((B, B), F32),
            V((64, B), F32),
            V((NZ, NX, NY, 32, B), BF),
            V((NZ, NY, NX, 32, B), BF),
            V((16, 16, B), F32),
            V((16, 16, B), F32),
            V((NZ, 16, B), F32),
            V((16, 16, B), F32),
            V((B, B), F32),
            dma((11,)),
            dma((5,)), dma((3,)), dma((NZ,)), dma((NZ,)),
            dma((2,)), dma((2,)), dma((2, 2)),
            dma(()), dma(()),
            dma((3,)), dma((3,)), dma((NZ,)),
            dma((2,)), dma((2,)),
            dma((2,)), dma((NZ,)),
            dma((2,)), dma((NZ,)), dma((NZ,)),
            dma((4,)), dma((NZ,)), dma((NZ,)),
            dma((3,)), dma((3,)),
            dma((4,)),
            pltpu.SemaphoreType.REGULAR,
        ],
        compiler_params=pltpu.CompilerParams(
            collective_id=0, has_side_effects=True, vmem_limit_bytes=60 * 2**20
        ),
        name="sage",
    )(features, w_self, w_neigh, tiles, dest.reshape(1, B), outside.reshape(1, B), cotangent)
    results = pl.pallas_call(
        hand_out,
        out_shape=tuple(jax.ShapeDtypeStruct(r.shape, t) for r, t in zip((results[0],) + results[2:], (BF, BF, F32, F32))),
        in_specs=[hbm] * 5,
        out_specs=(hbm,) * 4,
        scratch_shapes=[V(r.shape, r.dtype) for r in results] + [V((B, B), BF), dma((2, 5))],
        compiler_params=pltpu.CompilerParams(vmem_limit_bytes=60 * 2**20),
        name="hand_out",
    )(*results)
    output, grad_input, grad_self, grad_neigh = results
    return output, grad_input, grad_self.reshape(B, B), grad_neigh.reshape(B, B)


def solution(mesh):
    placed = (
        P("dom", None),
        P(None, "feat"),
        P(None, "feat"),
        P("dom", None, None),
        P("dom", None),
        P("dom"),
        P("dom", "feat"),
    )
    return jax.shard_map(
        on_device,
        mesh=mesh,
        in_specs=placed,
        out_specs=(P("dom", "feat"), P("dom", None), P(None, "feat"), P(None, "feat")),
        check_vma=False,
    )
```

```python
import jax
import jax.numpy as jnp
from jax import lax
from jax.experimental import pallas as pl
from jax.experimental.pallas import tpu as pltpu
from jax.sharding import PartitionSpec as P

MESH = pl.DeviceIdType.MESH
BF = jnp.bfloat16
F32 = jnp.float32
NX, NY, NZ = 4, 4, 8
B = 128
SPREAD = (2, 1, 3)
PLAN = ('s3', 's4', 't0', 's5', 's6', 'w2', 's7', 't3', 't4', 'r0', 't5', 't6', 't7', 'l0', 'w3', 'l3', 'l4', 'l5', 'l6', 'l1', 'l2', 'l7')


STEPS = (1, 7, 3, 5, 4, 2, 6, 0)
OWN = 7
PACKED = sum(step * 8**i for i, step in enumerate(STEPS))


def kernel(
    feat_h, ws_h, wn_h, tiles_h, dest_h, outside_h, cot_h,
    out_h, gis_h, gir_h, gs_h, gn_h,
    feat, ws, wn, dest, outside, cot, out_o, ws2, wn2, cot2,
    tiles, adj, xt, idx_v, idx_s, selfp, wnt, cott,
    sx, sy, r1x, r1y, p1x, p1y, r2x, r2y, rawx, rawy, rawl, rpx, rpy, p2x, p2y, r3,
    lk, rlk1, plk, rlk2, lk2, rlk3,
    gx, gy,
    w0, rw1, rw3, wg, gis,
    load_sem, s1, rraw, rs1x, rs1y, s2, rs2, rsp, s3, rs3, sl, rsl, rsl1, sg, rsg,
    sa, ra, sb, rbx, rby, sc, rcx, rcy, sw, rw, out_sem, past,
):
    dom = lax.axis_index("dom")
    c = lax.axis_index("feat")
    x = lax.rem(dom, NX)
    z = lax.rem(dom // NX, NZ)
    y = dom // (NX * NZ)
    oc = 1 - c

    def dev(px, py, pz, pc):
        return ((py * NZ + pz) * NX + px, pc)

    def xp(k):
        return lax.rem(x + k, NX)

    def yp(k):
        return lax.rem(y + k, NY)

    def zp(k):
        return lax.rem(z + k, NZ)

    def push(src, dst, send, recv, device):
        pltpu.make_async_remote_copy(
            src_ref=src, dst_ref=dst, send_sem=send, recv_sem=recv,
            device_id=device, device_id_type=MESH,
        ).start()

    def take(ref, sem):
        pltpu.make_async_copy(ref, ref, sem).wait()

    debts = []

    def owe(ref, sem):
        debts.append((ref, sem))

    def settle():
        for ref, sem in debts:
            take(ref, sem)

    loads = [
        pltpu.make_async_copy(src, dst, load_sem.at[i])
        for i, (src, dst) in enumerate(
            (
                (dest_h, dest), (feat_h, feat), (ws_h, ws),
                (wn_h, wn), (cot_h, cot), (outside_h, outside),
            )
        )
    ]
    for i in range(4):
        part = pl.ds(i * 32, 32)
        loads.append(pltpu.make_async_copy(tiles_h.at[part], tiles.at[part], load_sem.at[7 + i]))
    for load in loads:
        load.start()

    barrier = pltpu.get_barrier_semaphore()
    line = [dev(xp(k), y, z, c) for k in (1, 2, 3)] + [dev(x, yp(k), z, c) for k in (1, 2, 3)]
    line += [dev(x, y, zp(k), c) for k in range(1, NZ)] + [dev(x, y, z, oc)]
    for d in line:
        pl.semaphore_signal(barrier, inc=1, device_id=d, device_id_type=MESH)

    loads[0].wait()
    named = jnp.broadcast_to(dest[...], (B, B)).T
    lanes = lax.broadcasted_iota(jnp.int32, (B, B), 1)
    rows = lax.broadcasted_iota(jnp.int32, (B, B), 0)
    hit = named == lanes
    last = jnp.max(jnp.where(hit, rows, -1), axis=0, keepdims=True)
    first = jnp.min(jnp.where(hit, rows, B), axis=0, keepdims=True)
    idx_v[0:1, :] = first
    idx_v[1:2, :] = jnp.where(last > first, last, B)
    table = pltpu.make_async_copy(idx_v, idx_s, load_sem.at[6])
    table.start()
    tiles[B] = jnp.zeros((B, B), BF)
    loads[1].wait()
    features = feat[...]
    xt[0:B, :] = features.astype(F32).T.astype(BF)
    xh = xt[pl.ds(pl.multiple_of(c * 64, 64), 64), :]
    left = jnp.concatenate([xh, jnp.ones((16, B), BF)], axis=0)
    table.wait()
    for load in loads[6:]:
        load.wait()
    pl.semaphore_wait(barrier, len(line))
    pl.semaphore_signal(past, inc=1, device_id=dev(x, y, z, oc), device_id_type=MESH)

    for load in loads[2:5]:
        load.wait()
    for i, (mine, other) in enumerate(((ws, ws2), (wn, wn2), (cot, cot2))):
        push(mine, other, sg.at[i + 2], rsg.at[i], dev(x, y, z, oc))
        owe(mine, sg.at[i + 2])

    def partial_sums(p, dz):
        to_z = zp(dz)
        for py in range(NY):
            parts = []
            for px in range(NX):
                d = (py * NZ + to_z) * NX + px
                both = tiles[idx_s[0, d]] + tiles[idx_s[1, d]]
                adj[p, py, :, px * B:(px + 1) * B] = both
                parts.append(both)
            o = jnp.dot(left, jnp.concatenate(parts, axis=1), preferred_element_type=F32)
            for px in range(NX):
                part = o[:, px * B:(px + 1) * B]
                sx[p, px, py] = part[0:32].astype(BF)
                sy[p, py, px] = part[32:64].astype(BF)
                lk[p, px + c * (py - px), pl.ds(py + c * (px - py), 1), :] = part[64:65]

    def send_first(p):
        for k in SPREAD:
            push(sx.at[p, xp(k)], r1x.at[p, k - 1], s1.at[0], rs1x.at[p], dev(xp(k), y, z, c))
            push(sy.at[p, yp(k)], r1y.at[p, k - 1], s1.at[1], rs1y.at[p], dev(x, yp(k), z, c))
        for k in SPREAD:
            to = dev(x + oc * (xp(k) - x), y + c * (yp(k) - y), z, c)
            push(lk.at[p, xp(k) + c * (yp(k) - xp(k))], rlk1.at[p, k - 1], sl.at[0], rsl1.at[p], to)

    def to_next(p, code):
        dz = code % 8
        partial_sums(p, dz)
        to = dev(x, y, zp(dz), c)
        push(sx.at[p], rawx.at[p], s1.at[2], rraw.at[0], to)
        push(sy.at[p], rawy.at[p], s1.at[3], rraw.at[1], to)
        push(lk.at[p], rawl.at[p], s1.at[4], rraw.at[2], to)
        return code // 8

    def to_far(p, code):
        partial_sums(p, code % 8)
        send_first(p)
        return code // 8

    to_far(2, PACKED // 64)
    lax.fori_loop(0, 2, to_next, PACKED)
    lax.fori_loop(3, OWN, to_far, PACKED // 512)
    partial_sums(OWN, 0)

    def transposed(i, w_self, w_neigh, gradient):
        wnt[i] = w_neigh[...].astype(F32).T.astype(BF)
        cott[i] = gradient[...].astype(F32).T
        selfp[i] = jnp.dot(w_self[...].astype(F32).T.astype(BF), xt[...], preferred_element_type=F32)

    transposed(0, ws, wn, cot)

    def send_own():
        for sent, raw, i in ((sx, rawx, 0), (sy, rawy, 1)):
            take(raw, rraw.at[i])
            for k in range(4):
                total = sent[OWN, k].astype(F32) + raw[0, k].astype(F32) + raw[1, k].astype(F32)
                sent[OWN, k] = total.astype(BF)
        take(rawl, rraw.at[2])
        lk[OWN] = lk[OWN] + rawl[0] + rawl[1]
        send_first(OWN)

    def add_four(own, got):
        total = own.astype(F32)
        for k in range(3):
            total = total + got[k].astype(F32)
        return total

    joins = {5: 0, 6: 1}
    passed = {2: (1, 0), 3: (NZ - 1, 1)}
    slots = {4: 0, 5: 1, 6: 2}

    def sum_links(p):
        take(rlk1.at[p], rsl1.at[p])
        plk[p] = lk[p, x + c * (y - x)] + rlk1[p, 0] + rlk1[p, 1] + rlk1[p, 2]

    def second_phase(p):
        for share, own, got, sent, s_, r_, ready, passed_on, r_passed in (
            (0, sx.at[p, x], r1x, p1x, s2.at[0], r2x, rs1x, rpx, rsp),
            (1, sy.at[p, y], r1y, p1y, s2.at[1], r2y, rs1y, rpy, rsp),
        ):
            take(got.at[p], ready.at[p])
            total = add_four(own[...], got.at[p])
            if p in joins:
                take(passed_on.at[joins[p]], r_passed.at[share, joins[p]])
                total = total + passed_on[joins[p]].astype(F32)
            sent[p] = total.astype(BF)
            if p in passed:
                k, side = passed[p]
                push(sent.at[p], passed_on.at[side], s_, r_passed.at[share, side], dev(x, y, zp(k), c))
            else:
                push(sent.at[p], r_.at[slots[p]], s_, rs2.at[share], dev(x, y, zp(STEPS[p]), c))

    for p in range(2, OWN):
        second_phase(p)
        sum_links(p)
        push(plk.at[p], rlk2.at[p - 2], sl.at[1], rsl.at[1], dev(x, y, zp(STEPS[p]), c))
        if p == 4:
            send_own()
        if p == 4:
            for i, other in enumerate((ws2, wn2, cot2)):
                take(other, rsg.at[i])
            transposed(1, ws2, wn2, cot2)
    owe(sx.at[pl.ds(2, 6), pl.ds(0, 3)], s1.at[0])
    owe(sy.at[pl.ds(2, 6), pl.ds(0, 3)], s1.at[1])
    owe(rawx, s1.at[2])
    owe(rawy, s1.at[3])
    owe(rawl, s1.at[4])
    owe(lk.at[pl.ds(2, 6), pl.ds(0, 3)], sl.at[0])
    owe(p1x.at[pl.ds(0, 5)], s2.at[0])
    owe(p1y.at[pl.ds(0, 5)], s2.at[1])
    owe(plk.at[pl.ds(0, 5)], sl.at[1])
    own = OWN
    sum_links(own)
    take(r1x.at[own], rs1x.at[own])
    keep_x = add_four(sx[own, x], r1x.at[own])
    take(r1y.at[own], rs1y.at[own])
    keep_y = add_four(sy[own, y], r1y.at[own])

    pl.semaphore_wait(past, 1)
    take(r2x, rs2.at[0])
    for i in range(3):
        keep_x = keep_x + r2x[i].astype(F32)
    p2x[...] = keep_x.astype(BF)
    for pc in (c, oc):
        for k in SPREAD:
            push(p2x.at[yp(k)], r3.at[c * 4 + k], s3, rs3, dev(x, yp(k), z, pc))
    push(p2x.at[y], r3.at[c * 4], s3, rs3, dev(x, y, z, oc))
    take(r2y, rs2.at[1])
    for i in range(3):
        keep_y = keep_y + r2y[i].astype(F32)
    p2y[...] = keep_y.astype(BF)
    for pc in (c, oc):
        for k in SPREAD:
            push(p2y.at[xp(k)], r3.at[8 + c * 4 + k], s3, rs3, dev(xp(k), y, z, pc))
    push(p2y.at[x], r3.at[8 + c * 4], s3, rs3, dev(x, y, z, oc))
    take(rlk2, rsl.at[1])
    total = plk[own]
    for i in range(5):
        total = total + rlk2[i]
    lk2[...] = total
    for k in SPREAD:
        to = dev(x + c * (xp(k) - x), y + oc * (yp(k) - y), z, c)
        push(lk2, rlk3.at[k - 1], sl.at[2], rsl.at[2], to)
    r3[c * 4] = p2x[y]
    r3[8 + c * 4] = p2y[x]
    owe(r3.at[pl.ds(0, 14)], s3)
    owe(rlk3, sl.at[2])
    loads[5].wait()
    take(rlk3, rsl.at[2])
    row = pl.ds(y + c * (x - y), 1)
    links = lk2[row, :]
    for k in range(3):
        links = links + rlk3[k, row, :]
    inverse = 1.0 / (links + outside[...].astype(F32))
    take(r3.at[pl.ds(0, 14)], rs3)
    pieces = []
    for pc in range(2):
        for share in range(2):
            slot = share * 8 + pc * 4
            piece = r3[slot].astype(F32)
            for k in range(1, 4):
                piece = piece + r3[slot + k].astype(F32)
            pieces.append(piece)
    mean_t = jnp.concatenate(pieces, axis=0) * inverse
    mean_tb = mean_t.astype(BF)

    def layer(i):
        pre = selfp[i] + jnp.dot(wnt[i], mean_tb, preferred_element_type=F32)
        sigma = jax.nn.sigmoid(pre)
        return pre * sigma, (cott[i] * sigma * (1.0 + pre * (1.0 - sigma))).astype(BF)

    across = (((1,), (1,)), ((), ()))
    half = pl.ds(pl.multiple_of(c * 64, 64), 64)
    result, dpre_t = layer(0)
    _, other_t = layer(1)
    gfull = jnp.dot(wn[half, :], dpre_t, preferred_element_type=F32)
    gfull = gfull + jnp.dot(wn2[half, :], other_t, preferred_element_type=F32)
    gfull = (gfull * inverse).astype(BF)
    gx[0, x, y] = gfull[0:32]
    gy[0, y, x] = gfull[32:64]

    near = (0, 7, 1, 6, 2, 5, 3, 4)
    for k in SPREAD:
        push(gx.at[0, x, y], gx.at[0, x, y], sb.at[0], rbx.at[0], dev(x, yp(k), z, c))
        push(gy.at[0, y, x], gy.at[0, y, x], sb.at[1], rby.at[0], dev(xp(k), y, z, c))
    for q in range(3, NZ):
        to = dev(x, y, zp(NZ - near[q]), c)
        push(gx.at[0, x, y], gx.at[q, x, y], sa.at[0], ra.at[q], to)
        push(gy.at[0, y, x], gy.at[q, y, x], sa.at[1], ra.at[q], to)
    owe(gx.at[pl.ds(0, 5), 0, 0], sa.at[0])
    owe(gy.at[pl.ds(0, 5), 0, 0], sa.at[1])

    dpre = dpre_t.astype(F32).T.astype(BF)
    grad_s = jnp.dot(xt[...], dpre, preferred_element_type=F32)
    grad_n = jnp.dot(mean_tb, dpre, preferred_element_type=F32)
    w0[:, 0:8, :] = grad_s.reshape(16, 8, B)
    w0[:, 8:16, :] = grad_n.reshape(16, 8, B)
    here = x * NY + y
    plane = [(i, j) for i in (2, 1, 3, 0) for j in (2, 1, 3, 0) if (i, j) != (0, 0)]
    for i, j in plane:
        push(w0.at[xp(i) * NY + yp(j)], rw1.at[here], sw.at[0], rw.at[0], dev(xp(i), yp(j), z, c))
    owe(rw1.at[pl.ds(0, 15)], sw.at[0])
    direct = lax.dot_general(dpre, ws[...], across, preferred_element_type=F32)
    out_o[...] = result.T.astype(BF)
    emit = [pltpu.make_async_copy(out_o, out_h, out_sem.at[0])]
    emit[0].start()

    def across_second(q):
        take(gx.at[q, x, pl.ds(0, 2)], ra.at[q])
        for k in SPREAD:
            push(gx.at[q, x, y], gx.at[q, x, y], sb.at[0], rbx.at[q], dev(x, yp(k), z, c))
            push(gy.at[q, y, x], gy.at[q, y, x], sb.at[1], rby.at[q], dev(xp(k), y, z, c))

    def across_third(q):
        take(gx.at[q, x, pl.ds(0, 3)], rbx.at[q])
        for k in SPREAD:
            push(gx.at[q, x], gx.at[q, x], sc.at[0], rcx.at[q], dev(xp(k), y, z, c))
        take(gy.at[q, y, pl.ds(0, 3)], rby.at[q])
        for k in SPREAD:
            push(gy.at[q, y], gy.at[q, y], sc.at[1], rcy.at[q], dev(x, yp(k), z, c))

    def plane_to_next():
        take(gx.at[0, pl.ds(0, 3)], rcx.at[0])
        take(gy.at[0, pl.ds(0, 3)], rcy.at[0])
        for q in (1, 2):
            to = dev(x, y, zp(NZ - near[q]), c)
            push(gx.at[0], gx.at[q], sc.at[2], rbx.at[q], to)
            push(gy.at[0], gy.at[q], sc.at[3], rby.at[q], to)

    def last_phase(q, acc):
        if q in (1, 2):
            take(gx.at[q], rbx.at[q])
            take(gy.at[q], rby.at[q])
        elif q > 2:
            take(gx.at[q, pl.ds(0, 3)], rcx.at[q])
            take(gy.at[q, pl.ds(0, 3)], rcy.at[q])
        for py in range(NY):
            right = jnp.concatenate(
                [jnp.concatenate([gx[q, px, py], gy[q, py, px]], axis=0) for px in range(NX)], axis=1
            )
            acc = acc + lax.dot_general(adj[STEPS.index(near[q]), py], right, across, preferred_element_type=F32)
        return acc

    def weights_second():
        rw1[here] = w0[here]
        take(rw1.at[pl.ds(0, 15)], rw.at[0])
        total = rw1[0]
        for k in range(1, 16):
            total = total + rw1[k]
        rw3[z] = total
        for k in range(1, NZ):
            push(rw3.at[z], rw3.at[z], sw.at[1], rw.at[1], dev(x, y, zp(k), c))
        owe(rw3.at[pl.ds(0, 7)], sw.at[1])

    def weights_third():
        take(rw3.at[pl.ds(0, 7)], rw.at[1])
        total = rw3[0]
        for k in range(1, NZ):
            total = total + rw3[k]
        wg[...] = total
        for i, j in plane:
            to = dev(xp(i), yp(j), z, c)
            push(wg.at[pl.ds(0, 8)], gs_h.at[here], sw.at[2], rw.at[2], to)
            push(wg.at[pl.ds(8, 8)], gn_h.at[here], sw.at[2], rw.at[2], to)
        owe(rw1.at[pl.ds(0, 15)], sw.at[2])
        emit.append(pltpu.make_async_copy(wg.at[pl.ds(0, 8)], gs_h.at[here], out_sem.at[1]))
        emit.append(pltpu.make_async_copy(wg.at[pl.ds(8, 8)], gn_h.at[here], out_sem.at[2]))
        emit[1].start()
        emit[2].start()

    acc = jnp.zeros((B, 64), F32)
    weights = {2: weights_second, 3: weights_third}
    for step in PLAN:
        what, q = step[0], int(step[1])
        if what == "s":
            across_second(q)
        elif what == "t":
            across_third(q)
        elif what == "w":
            weights[q]()
        elif what == "r":
            plane_to_next()
        else:
            acc = last_phase(q, acc)
    owe(gx.at[pl.ds(0, 6), 0, pl.ds(0, 3)], sb.at[0])
    owe(gy.at[pl.ds(0, 6), 0, pl.ds(0, 3)], sb.at[1])
    owe(gx.at[pl.ds(0, 6), pl.ds(0, 3)], sc.at[0])
    owe(gy.at[pl.ds(0, 6), pl.ds(0, 3)], sc.at[1])
    owe(gx.at[pl.ds(0, 2)], sc.at[2])
    owe(gy.at[pl.ds(0, 2)], sc.at[3])

    none = jnp.zeros((B, 64), F32)
    placed = jnp.where(c == 0, jnp.concatenate([acc, none], axis=1), jnp.concatenate([none, acc], axis=1))
    gis[...] = placed + direct
    push(gis, gir_h, sg.at[1], rsg.at[3], dev(x, y, z, oc))
    emit.append(pltpu.make_async_copy(gis, gis_h, out_sem.at[3]))
    emit[3].start()
    take(rw1.at[pl.ds(0, 15)], rw.at[2])

    settle()
    take(gis, rsg.at[3])
    take(gis, sg.at[1])
    for copy in emit:
        copy.wait()


def hand_out(out_h, gis_h, gir_h, gs_h, gn_h, out_t, gi_t, gs_t, gn_t, out, gis, gir, gs, gn, gi, sems):
    inward = [
        pltpu.make_async_copy(a, b, sems.at[0, i])
        for i, (a, b) in enumerate(((gis_h, gis), (gir_h, gir), (out_h, out), (gs_h, gs), (gn_h, gn)))
    ]
    outward = [
        pltpu.make_async_copy(a, b, sems.at[1, i])
        for i, (a, b) in enumerate(((gi, gi_t), (out, out_t), (gs, gs_t), (gn, gn_t)))
    ]
    for copy in inward:
        copy.start()
    inward[0].wait()
    inward[1].wait()
    gi[...] = (gis[...] + gir[...]).astype(BF)
    outward[0].start()
    for first, second in zip(inward[2:], outward[1:]):
        first.wait()
        second.start()
    for copy in outward:
        copy.wait()


def on_device(features, w_self, w_neigh, tiles, dest, outside, cotangent):
    hbm = pl.BlockSpec(memory_space=pltpu.HBM)
    dma = pltpu.SemaphoreType.DMA
    V = pltpu.VMEM
    results = pl.pallas_call(
        kernel,
        out_shape=(
            jax.ShapeDtypeStruct((B, B), BF),
            jax.ShapeDtypeStruct((B, B), F32),
            jax.ShapeDtypeStruct((B, B), F32),
            jax.ShapeDtypeStruct((16, 8, B), F32),
            jax.ShapeDtypeStruct((16, 8, B), F32),
        ),
        in_specs=[hbm] * 7,
        out_specs=(hbm,) * 5,
        scratch_shapes=[
            V((B, B), BF), V((B, B), BF), V((B, B), BF), V((1, B), jnp.int32), V((1, B), jnp.int32),
            V((B, B), BF), V((B, B), BF),
            V((B, B), BF), V((B, B), BF), V((B, B), BF),
            V((B + 1, B, B), BF),
            V((NZ, NY, B, NX * B), BF),
            V((B, B), BF),
            V((8, B), jnp.int32),
            pltpu.SMEM((8, B), jnp.int32),
            V((2, B, B), F32),
            V((2, B, B), BF),
            V((2, B, B), F32),
            V((NZ, NX, NY, 32, B), BF),
            V((NZ, NY, NX, 32, B), BF),
            V((NZ, 3, NY, 32, B), BF),
            V((NZ, 3, NX, 32, B), BF),
            V((NZ, NY, 32, B), BF),
            V((NZ, NX, 32, B), BF),
            V((3, NY, 32, B), BF),
            V((3, NX, 32, B), BF),
            V((2, NX, NY, 32, B), BF),
            V((2, NY, NX, 32, B), BF),
            V((2, NX, 4, B), F32),
            V((2, NY, 32, B), BF),
            V((2, NX, 32, B), BF),
            V((NY, 32, B), BF),
            V((NX, 32, B), BF),
            V((16, 32, B), BF),
            V((NZ, NX, 4, B), F32),
            V((NZ, 3, 4, B), F32),
            V((NZ, 4, B), F32),
            V((5, 4, B), F32),
            V((4, B), F32),
            V((3, 4, B), F32),
            V((NZ, NX, NY, 32, B), BF),
            V((NZ, NY, NX, 32, B), BF),
            V((16, 16, B), F32),
            V((16, 16, B), F32),
            V((NZ, 16, B), F32),
            V((16, B), F32),
            V((B, B), F32),
            dma((11,)),
            dma((5,)), dma((3,)), dma((NZ,)), dma((NZ,)),
            dma((2,)), dma((2,)), dma((2, 2)),
            dma(()), dma(()),
            dma((3,)), dma((3,)), dma((NZ,)),
            dma((5,)), dma((4,)),
            dma((2,)), dma((NZ,)),
            dma((2,)), dma((NZ,)), dma((NZ,)),
            dma((4,)), dma((NZ,)), dma((NZ,)),
            dma((3,)), dma((3,)),
            dma((4,)),
            pltpu.SemaphoreType.REGULAR,
        ],
        compiler_params=pltpu.CompilerParams(
            collective_id=0, has_side_effects=True, vmem_limit_bytes=60 * 2**20
        ),
        name="sage",
    )(features, w_self, w_neigh, tiles, dest.reshape(1, B), outside.reshape(1, B), cotangent)
    results = pl.pallas_call(
        hand_out,
        out_shape=tuple(jax.ShapeDtypeStruct(r.shape, t) for r, t in zip((results[0],) + results[2:], (BF, BF, F32, F32))),
        in_specs=[hbm] * 5,
        out_specs=(hbm,) * 4,
        scratch_shapes=[V(r.shape, r.dtype) for r in results] + [V((B, B), BF), dma((2, 5))],
        compiler_params=pltpu.CompilerParams(vmem_limit_bytes=60 * 2**20),
        name="hand_out",
    )(*results)
    output, grad_input, grad_self, grad_neigh = results
    return output, grad_input, grad_self.reshape(B, B), grad_neigh.reshape(B, B)


def solution(mesh):
    placed = (
        P("dom", None),
        P(None, "feat"),
        P(None, "feat"),
        P("dom", None, None),
        P("dom", None),
        P("dom"),
        P("dom", "feat"),
    )
    return jax.shard_map(
        on_device,
        mesh=mesh,
        in_specs=placed,
        out_specs=(P("dom", "feat"), P("dom", None), P(None, "feat"), P(None, "feat")),
        check_vma=False,
    )
```

```python
import jax
import jax.numpy as jnp
from jax import lax
from jax.experimental import pallas as pl
from jax.experimental.pallas import tpu as pltpu
from jax.sharding import PartitionSpec as P

MESH = pl.DeviceIdType.MESH
BF = jnp.bfloat16
F32 = jnp.float32
NX, NY, NZ = 4, 4, 8
B = 128
SPREAD = (2, 1, 3)
PLAN = ('t0', 's3', 's4', 's5', 's6', 'w2', 't3', 's7', 't4', 'r0', 't5', 't6', 't7', 'l0', 'w3', 'l3', 'l4', 'l5', 'l6', 'l1', 'l2', 'l7')


STEPS = (1, 7, 3, 5, 4, 2, 6, 0)
OWN = 7
PACKED = sum(step * 8**i for i, step in enumerate(STEPS))


def kernel(
    feat_h, ws_h, wn_h, tiles_h, dest_h, outside_h, cot_h,
    out_h, gis_h, gir_h, gs_h, gn_h,
    feat, ws, wn, dest, outside, cot, out_o, ws2, wn2, cot2,
    tiles, adj, xt, idx_v, idx_s, selfp, wnt, cott,
    sx, sy, r1x, r1y, p1x, p1y, r2x, r2y, rawx, rawy, rawl, rpx, rpy, p2x, p2y, r3,
    lk, rlk1, plk, rlk2, lk2, rlk3,
    gx, gy,
    w0, rw1, rw3, wg, gis,
    load_sem, s1, rraw, rs1x, rs1y, s2, rs2, rsp, s3, rs3, sl, rsl, rsl1, sg, rsg,
    sa, ra, sb, rbx, rby, sc, rcx, rcy, sw, rw, out_sem, past,
):
    dom = lax.axis_index("dom")
    c = lax.axis_index("feat")
    x = lax.rem(dom, NX)
    z = lax.rem(dom // NX, NZ)
    y = dom // (NX * NZ)
    oc = 1 - c

    def dev(px, py, pz, pc):
        return ((py * NZ + pz) * NX + px, pc)

    def xp(k):
        return lax.rem(x + k, NX)

    def yp(k):
        return lax.rem(y + k, NY)

    def zp(k):
        return lax.rem(z + k, NZ)

    def push(src, dst, send, recv, device):
        pltpu.make_async_remote_copy(
            src_ref=src, dst_ref=dst, send_sem=send, recv_sem=recv,
            device_id=device, device_id_type=MESH,
        ).start()

    def take(ref, sem):
        pltpu.make_async_copy(ref, ref, sem).wait()

    debts = []

    def owe(ref, sem):
        debts.append((ref, sem))

    def settle():
        for ref, sem in debts:
            take(ref, sem)

    loads = [
        pltpu.make_async_copy(src, dst, load_sem.at[i])
        for i, (src, dst) in enumerate(
            (
                (dest_h, dest), (feat_h, feat), (ws_h, ws),
                (wn_h, wn), (cot_h, cot), (outside_h, outside),
            )
        )
    ]
    for i in range(4):
        part = pl.ds(i * 32, 32)
        loads.append(pltpu.make_async_copy(tiles_h.at[part], tiles.at[part], load_sem.at[7 + i]))
    for load in loads[6:] + loads[:6]:
        load.start()

    barrier = pltpu.get_barrier_semaphore()
    line = [dev(xp(k), y, z, c) for k in (1, 2, 3)] + [dev(x, yp(k), z, c) for k in (1, 2, 3)]
    line += [dev(x, y, zp(k), c) for k in range(1, NZ)] + [dev(x, y, z, oc)]
    for d in line:
        pl.semaphore_signal(barrier, inc=1, device_id=d, device_id_type=MESH)

    loads[0].wait()
    named = jnp.broadcast_to(dest[...], (B, B)).T
    lanes = lax.broadcasted_iota(jnp.int32, (B, B), 1)
    rows = lax.broadcasted_iota(jnp.int32, (B, B), 0)
    hit = named == lanes
    last = jnp.max(jnp.where(hit, rows, -1), axis=0, keepdims=True)
    first = jnp.min(jnp.where(hit, rows, B), axis=0, keepdims=True)
    idx_v[0:1, :] = first
    idx_v[1:2, :] = jnp.where(last > first, last, B)
    table = pltpu.make_async_copy(idx_v, idx_s, load_sem.at[6])
    table.start()
    tiles[B] = jnp.zeros((B, B), BF)
    loads[1].wait()
    features = feat[...]
    xt[0:B, :] = features.astype(F32).T.astype(BF)
    xh = xt[pl.ds(pl.multiple_of(c * 64, 64), 64), :]
    left = jnp.concatenate([xh, jnp.ones((16, B), BF)], axis=0)
    table.wait()
    for load in loads[6:]:
        load.wait()
    pl.semaphore_wait(barrier, len(line))
    pl.semaphore_signal(past, inc=1, device_id=dev(x, y, z, oc), device_id_type=MESH)

    for load in loads[2:5]:
        load.wait()
    for i, (mine, other) in enumerate(((ws, ws2), (wn, wn2), (cot, cot2))):
        push(mine, other, sg.at[i + 2], rsg.at[i], dev(x, y, z, oc))
        owe(mine, sg.at[i + 2])

    def partial_sums(p, dz):
        to_z = zp(dz)
        for py in range(NY):
            parts = []
            for px in range(NX):
                d = (py * NZ + to_z) * NX + px
                both = tiles[idx_s[0, d]] + tiles[idx_s[1, d]]
                adj[p, py, :, px * B:(px + 1) * B] = both
                parts.append(both)
            o = jnp.dot(left, jnp.concatenate(parts, axis=1), preferred_element_type=F32)
            for px in range(NX):
                part = o[:, px * B:(px + 1) * B]
                sx[p, px, py] = part[0:32].astype(BF)
                sy[p, py, px] = part[32:64].astype(BF)
                lk[p, px + c * (py - px), pl.ds(py + c * (px - py), 1), :] = part[64:65]

    def send_first(p):
        for k in SPREAD:
            push(sx.at[p, xp(k)], r1x.at[p, k - 1], s1.at[0], rs1x.at[p], dev(xp(k), y, z, c))
            push(sy.at[p, yp(k)], r1y.at[p, k - 1], s1.at[1], rs1y.at[p], dev(x, yp(k), z, c))
        for k in SPREAD:
            to = dev(x + oc * (xp(k) - x), y + c * (yp(k) - y), z, c)
            push(lk.at[p, xp(k) + c * (yp(k) - xp(k))], rlk1.at[p, k - 1], sl.at[0], rsl1.at[p], to)

    def to_next(p, code):
        dz = code % 8
        partial_sums(p, dz)
        to = dev(x, y, zp(dz), c)
        push(sx.at[p], rawx.at[p], s1.at[2], rraw.at[0], to)
        push(sy.at[p], rawy.at[p], s1.at[3], rraw.at[1], to)
        push(lk.at[p], rawl.at[p], s1.at[4], rraw.at[2], to)
        return code // 8

    def to_far(p, code):
        partial_sums(p, code % 8)
        send_first(p)
        return code // 8

    to_far(2, PACKED // 64)
    lax.fori_loop(0, 2, to_next, PACKED)
    lax.fori_loop(3, OWN, to_far, PACKED // 512)
    partial_sums(OWN, 0)

    def transposed(i, w_self, w_neigh, gradient):
        wnt[i] = w_neigh[...].astype(F32).T.astype(BF)
        cott[i] = gradient[...].astype(F32).T
        selfp[i] = jnp.dot(w_self[...].astype(F32).T.astype(BF), xt[...], preferred_element_type=F32)

    transposed(0, ws, wn, cot)

    def send_own():
        for sent, raw, i in ((sx, rawx, 0), (sy, rawy, 1)):
            take(raw, rraw.at[i])
            for k in range(4):
                total = sent[OWN, k].astype(F32) + raw[0, k].astype(F32) + raw[1, k].astype(F32)
                sent[OWN, k] = total.astype(BF)
        take(rawl, rraw.at[2])
        lk[OWN] = lk[OWN] + rawl[0] + rawl[1]
        send_first(OWN)

    def add_four(own, got):
        total = own.astype(F32)
        for k in range(3):
            total = total + got[k].astype(F32)
        return total

    joins = {5: 0, 6: 1}
    passed = {2: (1, 0), 3: (NZ - 1, 1)}
    slots = {4: 0, 5: 1, 6: 2}

    def sum_links(p):
        take(rlk1.at[p], rsl1.at[p])
        plk[p] = lk[p, x + c * (y - x)] + rlk1[p, 0] + rlk1[p, 1] + rlk1[p, 2]

    def second_phase(p):
        for share, own, got, sent, s_, r_, ready, passed_on, r_passed in (
            (0, sx.at[p, x], r1x, p1x, s2.at[0], r2x, rs1x, rpx, rsp),
            (1, sy.at[p, y], r1y, p1y, s2.at[1], r2y, rs1y, rpy, rsp),
        ):
            take(got.at[p], ready.at[p])
            total = add_four(own[...], got.at[p])
            if p in joins:
                take(passed_on.at[joins[p]], r_passed.at[share, joins[p]])
                total = total + passed_on[joins[p]].astype(F32)
            sent[p] = total.astype(BF)
            if p in passed:
                k, side = passed[p]
                push(sent.at[p], passed_on.at[side], s_, r_passed.at[share, side], dev(x, y, zp(k), c))
            else:
                push(sent.at[p], r_.at[slots[p]], s_, rs2.at[share], dev(x, y, zp(STEPS[p]), c))

    for p in range(2, OWN):
        second_phase(p)
        sum_links(p)
        push(plk.at[p], rlk2.at[p - 2], sl.at[1], rsl.at[1], dev(x, y, zp(STEPS[p]), c))
        if p == 4:
            send_own()
        if p == 4:
            for i, other in enumerate((ws2, wn2, cot2)):
                take(other, rsg.at[i])
            transposed(1, ws2, wn2, cot2)
    owe(sx.at[pl.ds(2, 6), pl.ds(0, 3)], s1.at[0])
    owe(sy.at[pl.ds(2, 6), pl.ds(0, 3)], s1.at[1])
    owe(rawx, s1.at[2])
    owe(rawy, s1.at[3])
    owe(rawl, s1.at[4])
    owe(lk.at[pl.ds(2, 6), pl.ds(0, 3)], sl.at[0])
    owe(p1x.at[pl.ds(0, 5)], s2.at[0])
    owe(p1y.at[pl.ds(0, 5)], s2.at[1])
    owe(plk.at[pl.ds(0, 5)], sl.at[1])
    own = OWN
    sum_links(own)
    take(r1x.at[own], rs1x.at[own])
    keep_x = add_four(sx[own, x], r1x.at[own])
    take(r1y.at[own], rs1y.at[own])
    keep_y = add_four(sy[own, y], r1y.at[own])

    pl.semaphore_wait(past, 1)
    take(r2x, rs2.at[0])
    for i in range(3):
        keep_x = keep_x + r2x[i].astype(F32)
    p2x[...] = keep_x.astype(BF)
    for pc in (c, oc):
        for k in SPREAD:
            push(p2x.at[yp(k)], r3.at[c * 4 + k], s3, rs3, dev(x, yp(k), z, pc))
    push(p2x.at[y], r3.at[c * 4], s3, rs3, dev(x, y, z, oc))
    take(r2y, rs2.at[1])
    for i in range(3):
        keep_y = keep_y + r2y[i].astype(F32)
    p2y[...] = keep_y.astype(BF)
    for pc in (c, oc):
        for k in SPREAD:
            push(p2y.at[xp(k)], r3.at[8 + c * 4 + k], s3, rs3, dev(xp(k), y, z, pc))
    push(p2y.at[x], r3.at[8 + c * 4], s3, rs3, dev(x, y, z, oc))
    take(rlk2, rsl.at[1])
    total = plk[own]
    for i in range(5):
        total = total + rlk2[i]
    lk2[...] = total
    for k in SPREAD:
        to = dev(x + c * (xp(k) - x), y + oc * (yp(k) - y), z, c)
        push(lk2, rlk3.at[k - 1], sl.at[2], rsl.at[2], to)
    r3[c * 4] = p2x[y]
    r3[8 + c * 4] = p2y[x]
    owe(r3.at[pl.ds(0, 14)], s3)
    owe(rlk3, sl.at[2])
    loads[5].wait()
    take(rlk3, rsl.at[2])
    row = pl.ds(y + c * (x - y), 1)
    links = lk2[row, :]
    for k in range(3):
        links = links + rlk3[k, row, :]
    inverse = 1.0 / (links + outside[...].astype(F32))
    take(r3.at[pl.ds(0, 14)], rs3)
    pieces = []
    for pc in range(2):
        for share in range(2):
            slot = share * 8 + pc * 4
            piece = r3[slot].astype(F32)
            for k in range(1, 4):
                piece = piece + r3[slot + k].astype(F32)
            pieces.append(piece)
    mean_t = jnp.concatenate(pieces, axis=0) * inverse
    mean_tb = mean_t.astype(BF)

    def layer(i):
        pre = selfp[i] + jnp.dot(wnt[i], mean_tb, preferred_element_type=F32)
        sigma = jax.nn.sigmoid(pre)
        return pre * sigma, (cott[i] * sigma * (1.0 + pre * (1.0 - sigma))).astype(BF)

    across = (((1,), (1,)), ((), ()))
    half = pl.ds(pl.multiple_of(c * 64, 64), 64)
    result, dpre_t = layer(0)
    _, other_t = layer(1)
    gfull = jnp.dot(wn[half, :], dpre_t, preferred_element_type=F32)
    gfull = gfull + jnp.dot(wn2[half, :], other_t, preferred_element_type=F32)
    gfull = (gfull * inverse).astype(BF)
    gx[0, x, y] = gfull[0:32]
    gy[0, y, x] = gfull[32:64]

    near = (0, 7, 1, 6, 2, 5, 3, 4)
    for k in SPREAD:
        push(gx.at[0, x, y], gx.at[0, x, y], sb.at[0], rbx.at[0], dev(x, yp(k), z, c))
        push(gy.at[0, y, x], gy.at[0, y, x], sb.at[1], rby.at[0], dev(xp(k), y, z, c))
    for q in range(3, NZ):
        to = dev(x, y, zp(NZ - near[q]), c)
        push(gx.at[0, x, y], gx.at[q, x, y], sa.at[0], ra.at[q], to)
        push(gy.at[0, y, x], gy.at[q, y, x], sa.at[1], ra.at[q], to)
    owe(gx.at[pl.ds(0, 5), 0, 0], sa.at[0])
    owe(gy.at[pl.ds(0, 5), 0, 0], sa.at[1])

    dpre = dpre_t.astype(F32).T.astype(BF)
    grad_s = jnp.dot(xt[...], dpre, preferred_element_type=F32)
    grad_n = jnp.dot(mean_tb, dpre, preferred_element_type=F32)
    w0[:, 0:8, :] = grad_s.reshape(16, 8, B)
    w0[:, 8:16, :] = grad_n.reshape(16, 8, B)
    here = x * NY + y
    plane = [(i, j) for i in (2, 1, 3, 0) for j in (2, 1, 3, 0) if (i, j) != (0, 0)]
    for i, j in plane:
        push(w0.at[xp(i) * NY + yp(j)], rw1.at[here], sw.at[0], rw.at[0], dev(xp(i), yp(j), z, c))
    owe(rw1.at[pl.ds(0, 15)], sw.at[0])
    direct = lax.dot_general(dpre, ws[...], across, preferred_element_type=F32)
    out_o[...] = result.T.astype(BF)
    emit = [pltpu.make_async_copy(out_o, out_h, out_sem.at[0])]
    emit[0].start()

    def across_second(q):
        take(gx.at[q, x, pl.ds(0, 2)], ra.at[q])
        for k in SPREAD:
            push(gx.at[q, x, y], gx.at[q, x, y], sb.at[0], rbx.at[q], dev(x, yp(k), z, c))
            push(gy.at[q, y, x], gy.at[q, y, x], sb.at[1], rby.at[q], dev(xp(k), y, z, c))

    def across_third(q):
        take(gx.at[q, x, pl.ds(0, 3)], rbx.at[q])
        for k in SPREAD:
            push(gx.at[q, x], gx.at[q, x], sc.at[0], rcx.at[q], dev(xp(k), y, z, c))
        take(gy.at[q, y, pl.ds(0, 3)], rby.at[q])
        for k in SPREAD:
            push(gy.at[q, y], gy.at[q, y], sc.at[1], rcy.at[q], dev(x, yp(k), z, c))

    def plane_to_next():
        take(gx.at[0, pl.ds(0, 3)], rcx.at[0])
        take(gy.at[0, pl.ds(0, 3)], rcy.at[0])
        for q in (1, 2):
            to = dev(x, y, zp(NZ - near[q]), c)
            push(gx.at[0], gx.at[q], sc.at[2], rbx.at[q], to)
            push(gy.at[0], gy.at[q], sc.at[3], rby.at[q], to)

    def last_phase(q, acc):
        if q in (1, 2):
            take(gx.at[q], rbx.at[q])
            take(gy.at[q], rby.at[q])
        elif q > 2:
            take(gx.at[q, pl.ds(0, 3)], rcx.at[q])
            take(gy.at[q, pl.ds(0, 3)], rcy.at[q])
        for py in range(NY):
            right = jnp.concatenate(
                [jnp.concatenate([gx[q, px, py], gy[q, py, px]], axis=0) for px in range(NX)], axis=1
            )
            acc = acc + lax.dot_general(adj[STEPS.index(near[q]), py], right, across, preferred_element_type=F32)
        return acc

    def weights_second():
        rw1[here] = w0[here]
        take(rw1.at[pl.ds(0, 15)], rw.at[0])
        total = rw1[0]
        for k in range(1, 16):
            total = total + rw1[k]
        rw3[z] = total
        for k in range(1, NZ):
            push(rw3.at[z], rw3.at[z], sw.at[1], rw.at[1], dev(x, y, zp(k), c))
        owe(rw3.at[pl.ds(0, 7)], sw.at[1])

    def weights_third():
        take(rw3.at[pl.ds(0, 7)], rw.at[1])
        total = rw3[0]
        for k in range(1, NZ):
            total = total + rw3[k]
        wg[...] = total
        for i, j in plane:
            to = dev(xp(i), yp(j), z, c)
            push(wg.at[pl.ds(0, 8)], gs_h.at[here], sw.at[2], rw.at[2], to)
            push(wg.at[pl.ds(8, 8)], gn_h.at[here], sw.at[2], rw.at[2], to)
        owe(rw1.at[pl.ds(0, 15)], sw.at[2])
        emit.append(pltpu.make_async_copy(wg.at[pl.ds(0, 8)], gs_h.at[here], out_sem.at[1]))
        emit.append(pltpu.make_async_copy(wg.at[pl.ds(8, 8)], gn_h.at[here], out_sem.at[2]))
        emit[1].start()
        emit[2].start()

    acc = jnp.zeros((B, 64), F32)
    weights = {2: weights_second, 3: weights_third}
    for step in PLAN:
        what, q = step[0], int(step[1])
        if what == "s":
            across_second(q)
        elif what == "t":
            across_third(q)
        elif what == "w":
            weights[q]()
        elif what == "r":
            plane_to_next()
        else:
            acc = last_phase(q, acc)
    owe(gx.at[pl.ds(0, 6), 0, pl.ds(0, 3)], sb.at[0])
    owe(gy.at[pl.ds(0, 6), 0, pl.ds(0, 3)], sb.at[1])
    owe(gx.at[pl.ds(0, 6), pl.ds(0, 3)], sc.at[0])
    owe(gy.at[pl.ds(0, 6), pl.ds(0, 3)], sc.at[1])
    owe(gx.at[pl.ds(0, 2)], sc.at[2])
    owe(gy.at[pl.ds(0, 2)], sc.at[3])

    none = jnp.zeros((B, 64), F32)
    placed = jnp.where(c == 0, jnp.concatenate([acc, none], axis=1), jnp.concatenate([none, acc], axis=1))
    gis[...] = placed + direct
    push(gis, gir_h, sg.at[1], rsg.at[3], dev(x, y, z, oc))
    emit.append(pltpu.make_async_copy(gis, gis_h, out_sem.at[3]))
    emit[3].start()
    take(rw1.at[pl.ds(0, 15)], rw.at[2])

    settle()
    take(gis, rsg.at[3])
    take(gis, sg.at[1])
    for copy in emit:
        copy.wait()


def hand_out(out_h, gis_h, gir_h, gs_h, gn_h, out_t, gi_t, gs_t, gn_t, out, gis, gir, gs, gn, gi, sems):
    inward = [
        pltpu.make_async_copy(a, b, sems.at[0, i])
        for i, (a, b) in enumerate(((gis_h, gis), (gir_h, gir), (out_h, out), (gs_h, gs), (gn_h, gn)))
    ]
    outward = [
        pltpu.make_async_copy(a, b, sems.at[1, i])
        for i, (a, b) in enumerate(((gi, gi_t), (out, out_t), (gs, gs_t), (gn, gn_t)))
    ]
    for copy in inward:
        copy.start()
    inward[0].wait()
    inward[1].wait()
    gi[...] = (gis[...] + gir[...]).astype(BF)
    outward[0].start()
    for first, second in zip(inward[2:], outward[1:]):
        first.wait()
        second.start()
    for copy in outward:
        copy.wait()


def on_device(features, w_self, w_neigh, tiles, dest, outside, cotangent):
    hbm = pl.BlockSpec(memory_space=pltpu.HBM)
    dma = pltpu.SemaphoreType.DMA
    V = pltpu.VMEM
    results = pl.pallas_call(
        kernel,
        out_shape=(
            jax.ShapeDtypeStruct((B, B), BF),
            jax.ShapeDtypeStruct((B, B), F32),
            jax.ShapeDtypeStruct((B, B), F32),
            jax.ShapeDtypeStruct((16, 8, B), F32),
            jax.ShapeDtypeStruct((16, 8, B), F32),
        ),
        in_specs=[hbm] * 7,
        out_specs=(hbm,) * 5,
        scratch_shapes=[
            V((B, B), BF), V((B, B), BF), V((B, B), BF), V((1, B), jnp.int32), V((1, B), jnp.int32),
            V((B, B), BF), V((B, B), BF),
            V((B, B), BF), V((B, B), BF), V((B, B), BF),
            V((B + 1, B, B), BF),
            V((NZ, NY, B, NX * B), BF),
            V((B, B), BF),
            V((8, B), jnp.int32),
            pltpu.SMEM((8, B), jnp.int32),
            V((2, B, B), F32),
            V((2, B, B), BF),
            V((2, B, B), F32),
            V((NZ, NX, NY, 32, B), BF),
            V((NZ, NY, NX, 32, B), BF),
            V((NZ, 3, NY, 32, B), BF),
            V((NZ, 3, NX, 32, B), BF),
            V((NZ, NY, 32, B), BF),
            V((NZ, NX, 32, B), BF),
            V((3, NY, 32, B), BF),
            V((3, NX, 32, B), BF),
            V((2, NX, NY, 32, B), BF),
            V((2, NY, NX, 32, B), BF),
            V((2, NX, 4, B), F32),
            V((2, NY, 32, B), BF),
            V((2, NX, 32, B), BF),
            V((NY, 32, B), BF),
            V((NX, 32, B), BF),
            V((16, 32, B), BF),
            V((NZ, NX, 4, B), F32),
            V((NZ, 3, 4, B), F32),
            V((NZ, 4, B), F32),
            V((5, 4, B), F32),
            V((4, B), F32),
            V((3, 4, B), F32),
            V((NZ, NX, NY, 32, B), BF),
            V((NZ, NY, NX, 32, B), BF),
            V((16, 16, B), F32),
            V((16, 16, B), F32),
            V((NZ, 16, B), F32),
            V((16, B), F32),
            V((B, B), F32),
            dma((11,)),
            dma((5,)), dma((3,)), dma((NZ,)), dma((NZ,)),
            dma((2,)), dma((2,)), dma((2, 2)),
            dma(()), dma(()),
            dma((3,)), dma((3,)), dma((NZ,)),
            dma((5,)), dma((4,)),
            dma((2,)), dma((NZ,)),
            dma((2,)), dma((NZ,)), dma((NZ,)),
            dma((4,)), dma((NZ,)), dma((NZ,)),
            dma((3,)), dma((3,)),
            dma((4,)),
            pltpu.SemaphoreType.REGULAR,
        ],
        compiler_params=pltpu.CompilerParams(
            collective_id=0, has_side_effects=True, vmem_limit_bytes=60 * 2**20
        ),
        name="sage",
    )(features, w_self, w_neigh, tiles, dest.reshape(1, B), outside.reshape(1, B), cotangent)
    results = pl.pallas_call(
        hand_out,
        out_shape=tuple(jax.ShapeDtypeStruct(r.shape, t) for r, t in zip((results[0],) + results[2:], (BF, BF, F32, F32))),
        in_specs=[hbm] * 5,
        out_specs=(hbm,) * 4,
        scratch_shapes=[V(r.shape, r.dtype) for r in results] + [V((B, B), BF), dma((2, 5))],
        compiler_params=pltpu.CompilerParams(vmem_limit_bytes=60 * 2**20),
        name="hand_out",
    )(*results)
    output, grad_input, grad_self, grad_neigh = results
    return output, grad_input, grad_self.reshape(B, B), grad_neigh.reshape(B, B)


def solution(mesh):
    placed = (
        P("dom", None),
        P(None, "feat"),
        P(None, "feat"),
        P("dom", None, None),
        P("dom", None),
        P("dom"),
        P("dom", "feat"),
    )
    return jax.shard_map(
        on_device,
        mesh=mesh,
        in_specs=placed,
        out_specs=(P("dom", "feat"), P("dom", None), P(None, "feat"), P(None, "feat")),
        check_vma=False,
    )
```

```python
import jax
import jax.numpy as jnp
from jax import lax
from jax.experimental import pallas as pl
from jax.experimental.pallas import tpu as pltpu
from jax.sharding import PartitionSpec as P

MESH = pl.DeviceIdType.MESH
BF = jnp.bfloat16
F32 = jnp.float32
NX, NY, NZ = 4, 4, 8
B = 128
SPREAD = (2, 1, 3)
PLAN = ('t0', 's3', 's4', 's5', 's6', 'w2', 't3', 's7', 't4', 'r0', 't5', 't6', 't7', 'l0', 'w3', 'l3', 'l4', 'l5', 'l6', 'l1', 'l2', 'l7')


STEPS = (1, 7, 3, 5, 4, 2, 6, 0)
OWN = 7
PACKED = sum(step * 8**i for i, step in enumerate(STEPS))


def kernel(
    feat_h, ws_h, wn_h, tiles_h, dest_h, outside_h, cot_h,
    out_h, gis_h, gir_h, gs_h, gn_h,
    feat, ws, wn, dest, outside, cot, out_o, ws2, wn2, cot2,
    tiles, adj, xt, idx_v, idx_s, selfp, wnt, cott,
    sx, sy, r1x, r1y, p1x, p1y, r2x, r2y, rawx, rawy, rawl, rpx, rpy, p2x, p2y, r3,
    lk, rlk1, plk, rlk2, lk2, rlk3,
    gx, gy,
    w0, rw1, rw3, wg, gis,
    load_sem, s1, rraw, rs1x, rs1y, s2, rs2, rsp, s3, rs3, sl, rsl, rsl1, sg, rsg,
    sa, ra, sb, rbx, rby, sc, rcx, rcy, sw, rw, out_sem, past,
):
    dom = lax.axis_index("dom")
    c = lax.axis_index("feat")
    x = lax.rem(dom, NX)
    z = lax.rem(dom // NX, NZ)
    y = dom // (NX * NZ)
    oc = 1 - c

    def dev(px, py, pz, pc):
        return ((py * NZ + pz) * NX + px, pc)

    def xp(k):
        return lax.rem(x + k, NX)

    def yp(k):
        return lax.rem(y + k, NY)

    def zp(k):
        return lax.rem(z + k, NZ)

    def push(src, dst, send, recv, device):
        pltpu.make_async_remote_copy(
            src_ref=src, dst_ref=dst, send_sem=send, recv_sem=recv,
            device_id=device, device_id_type=MESH,
        ).start()

    def take(ref, sem):
        pltpu.make_async_copy(ref, ref, sem).wait()

    debts = []

    def owe(ref, sem):
        debts.append((ref, sem))

    def settle():
        for ref, sem in debts:
            take(ref, sem)

    loads = [
        pltpu.make_async_copy(src, dst, load_sem.at[i])
        for i, (src, dst) in enumerate(
            (
                (dest_h, dest), (feat_h, feat), (ws_h, ws),
                (wn_h, wn), (cot_h, cot), (outside_h, outside),
            )
        )
    ]
    for i in range(4):
        part = pl.ds(i * 32, 32)
        loads.append(pltpu.make_async_copy(tiles_h.at[part], tiles.at[part], load_sem.at[7 + i]))
    for load in loads[6:] + loads[:6]:
        load.start()

    barrier = pltpu.get_barrier_semaphore()
    line = [dev(xp(k), y, z, c) for k in (1, 2, 3)] + [dev(x, yp(k), z, c) for k in (1, 2, 3)]
    line += [dev(x, y, zp(k), c) for k in range(1, NZ)] + [dev(x, y, z, oc)]
    for d in line:
        pl.semaphore_signal(barrier, inc=1, device_id=d, device_id_type=MESH)

    loads[0].wait()
    named = jnp.broadcast_to(dest[...], (B, B)).T
    lanes = lax.broadcasted_iota(jnp.int32, (B, B), 1)
    rows = lax.broadcasted_iota(jnp.int32, (B, B), 0)
    hit = named == lanes
    last = jnp.max(jnp.where(hit, rows, -1), axis=0, keepdims=True)
    first = jnp.min(jnp.where(hit, rows, B), axis=0, keepdims=True)
    idx_v[0:1, :] = first
    idx_v[1:2, :] = jnp.where(last > first, last, B)
    table = pltpu.make_async_copy(idx_v, idx_s, load_sem.at[6])
    table.start()
    tiles[B] = jnp.zeros((B, B), BF)
    loads[1].wait()
    features = feat[...]
    xt[0:B, :] = features.astype(F32).T.astype(BF)
    xh = xt[pl.ds(pl.multiple_of(c * 64, 64), 64), :]
    left = jnp.concatenate([xh, jnp.ones((16, B), BF)], axis=0)
    table.wait()
    for load in loads[6:]:
        load.wait()
    pl.semaphore_wait(barrier, len(line))
    pl.semaphore_signal(past, inc=1, device_id=dev(x, y, z, oc), device_id_type=MESH)

    for load in loads[2:5]:
        load.wait()
    for i, (mine, other) in enumerate(((ws, ws2), (wn, wn2), (cot, cot2))):
        push(mine, other, sg.at[i + 2], rsg.at[i], dev(x, y, z, oc))
        owe(mine, sg.at[i + 2])

    def partial_sums(p, dz):
        to_z = zp(dz)
        for py in range(NY):
            parts = []
            for px in range(NX):
                d = (py * NZ + to_z) * NX + px
                both = tiles[idx_s[0, d]] + tiles[idx_s[1, d]]
                adj[p, py, :, px * B:(px + 1) * B] = both
                parts.append(both)
            o = jnp.dot(left, jnp.concatenate(parts, axis=1), preferred_element_type=F32)
            for px in range(NX):
                part = o[:, px * B:(px + 1) * B]
                sx[p, px, py] = part[0:32].astype(BF)
                sy[p, py, px] = part[32:64].astype(BF)
                lk[p, px + c * (py - px), pl.ds(py + c * (px - py), 1), :] = part[64:65]

    def send_first(p):
        for k in SPREAD:
            push(sx.at[p, xp(k)], r1x.at[p, k - 1], s1.at[0], rs1x.at[p], dev(xp(k), y, z, c))
            push(sy.at[p, yp(k)], r1y.at[p, k - 1], s1.at[1], rs1y.at[p], dev(x, yp(k), z, c))
        for k in SPREAD:
            to = dev(x + oc * (xp(k) - x), y + c * (yp(k) - y), z, c)
            push(lk.at[p, xp(k) + c * (yp(k) - xp(k))], rlk1.at[p, k - 1], sl.at[0], rsl1.at[p], to)

    def to_next(p, code):
        dz = code % 8
        partial_sums(p, dz)
        to = dev(x, y, zp(dz), c)
        push(sx.at[p], rawx.at[p], s1.at[2], rraw.at[0], to)
        push(sy.at[p], rawy.at[p], s1.at[3], rraw.at[1], to)
        push(lk.at[p], rawl.at[p], s1.at[4], rraw.at[2], to)
        return code // 8

    def to_far(p, code):
        partial_sums(p, code % 8)
        send_first(p)
        return code // 8

    to_far(2, PACKED // 64)
    lax.fori_loop(0, 2, to_next, PACKED)
    lax.fori_loop(3, OWN, to_far, PACKED // 512)
    partial_sums(OWN, 0)

    def transposed(i, w_self, w_neigh, gradient):
        wnt[i] = w_neigh[...].astype(F32).T.astype(BF)
        cott[i] = gradient[...].astype(F32).T
        selfp[i] = jnp.dot(w_self[...].astype(F32).T.astype(BF), xt[...], preferred_element_type=F32)

    transposed(0, ws, wn, cot)

    def send_own():
        for sent, raw, i in ((sx, rawx, 0), (sy, rawy, 1)):
            take(raw, rraw.at[i])
            for k in range(4):
                total = sent[OWN, k].astype(F32) + raw[0, k].astype(F32) + raw[1, k].astype(F32)
                sent[OWN, k] = total.astype(BF)
        take(rawl, rraw.at[2])
        lk[OWN] = lk[OWN] + rawl[0] + rawl[1]
        send_first(OWN)

    def add_four(own, got):
        total = own.astype(F32)
        for k in range(3):
            total = total + got[k].astype(F32)
        return total

    joins = {5: 0, 6: 1}
    passed = {2: (1, 0), 3: (NZ - 1, 1)}
    slots = {4: 0, 5: 1, 6: 2}

    def sum_links(p):
        take(rlk1.at[p], rsl1.at[p])
        plk[p] = lk[p, x + c * (y - x)] + rlk1[p, 0] + rlk1[p, 1] + rlk1[p, 2]

    def second_phase(p):
        for share, own, got, sent, s_, r_, ready, passed_on, r_passed in (
            (0, sx.at[p, x], r1x, p1x, s2.at[0], r2x, rs1x, rpx, rsp),
            (1, sy.at[p, y], r1y, p1y, s2.at[1], r2y, rs1y, rpy, rsp),
        ):
            take(got.at[p], ready.at[p])
            total = add_four(own[...], got.at[p])
            if p in joins:
                take(passed_on.at[joins[p]], r_passed.at[share, joins[p]])
                total = total + passed_on[joins[p]].astype(F32)
            sent[p] = total.astype(BF)
            if p in passed:
                k, side = passed[p]
                push(sent.at[p], passed_on.at[side], s_, r_passed.at[share, side], dev(x, y, zp(k), c))
            else:
                push(sent.at[p], r_.at[slots[p]], s_, rs2.at[share], dev(x, y, zp(STEPS[p]), c))

    for p in range(2, OWN):
        second_phase(p)
        sum_links(p)
        push(plk.at[p], rlk2.at[p - 2], sl.at[1], rsl.at[1], dev(x, y, zp(STEPS[p]), c))
        if p == 4:
            send_own()
        if p == 4:
            for i, other in enumerate((ws2, wn2, cot2)):
                take(other, rsg.at[i])
            transposed(1, ws2, wn2, cot2)
    owe(sx.at[pl.ds(2, 6), pl.ds(0, 3)], s1.at[0])
    owe(sy.at[pl.ds(2, 6), pl.ds(0, 3)], s1.at[1])
    owe(rawx, s1.at[2])
    owe(rawy, s1.at[3])
    owe(rawl, s1.at[4])
    owe(lk.at[pl.ds(2, 6), pl.ds(0, 3)], sl.at[0])
    owe(p1x.at[pl.ds(0, 5)], s2.at[0])
    owe(p1y.at[pl.ds(0, 5)], s2.at[1])
    owe(plk.at[pl.ds(0, 5)], sl.at[1])
    own = OWN
    sum_links(own)
    take(r1x.at[own], rs1x.at[own])
    keep_x = add_four(sx[own, x], r1x.at[own])
    take(r1y.at[own], rs1y.at[own])
    keep_y = add_four(sy[own, y], r1y.at[own])

    pl.semaphore_wait(past, 1)
    take(r2x, rs2.at[0])
    for i in range(3):
        keep_x = keep_x + r2x[i].astype(F32)
    p2x[...] = keep_x.astype(BF)
    for pc in (c, oc):
        for k in SPREAD:
            push(p2x.at[yp(k)], r3.at[c * 4 + k], s3, rs3, dev(x, yp(k), z, pc))
    push(p2x.at[y], r3.at[c * 4], s3, rs3, dev(x, y, z, oc))
    take(r2y, rs2.at[1])
    for i in range(3):
        keep_y = keep_y + r2y[i].astype(F32)
    p2y[...] = keep_y.astype(BF)
    for pc in (c, oc):
        for k in SPREAD:
            push(p2y.at[xp(k)], r3.at[8 + c * 4 + k], s3, rs3, dev(xp(k), y, z, pc))
    push(p2y.at[x], r3.at[8 + c * 4], s3, rs3, dev(x, y, z, oc))
    take(rlk2, rsl.at[1])
    total = plk[own]
    for i in range(5):
        total = total + rlk2[i]
    lk2[...] = total
    for k in SPREAD:
        to = dev(x + c * (xp(k) - x), y + oc * (yp(k) - y), z, c)
        push(lk2, rlk3.at[k - 1], sl.at[2], rsl.at[2], to)
    r3[c * 4] = p2x[y]
    r3[8 + c * 4] = p2y[x]
    owe(r3.at[pl.ds(0, 14)], s3)
    owe(rlk3, sl.at[2])
    loads[5].wait()
    take(rlk3, rsl.at[2])
    row = pl.ds(y + c * (x - y), 1)
    links = lk2[row, :]
    for k in range(3):
        links = links + rlk3[k, row, :]
    inverse = 1.0 / (links + outside[...].astype(F32))
    take(r3.at[pl.ds(0, 14)], rs3)
    pieces = []
    for pc in range(2):
        for share in range(2):
            slot = share * 8 + pc * 4
            piece = r3[slot].astype(F32)
            for k in range(1, 4):
                piece = piece + r3[slot + k].astype(F32)
            pieces.append(piece)
    mean_t = jnp.concatenate(pieces, axis=0) * inverse
    mean_tb = mean_t.astype(BF)

    def layer(i):
        pre = selfp[i] + jnp.dot(wnt[i], mean_tb, preferred_element_type=F32)
        sigma = jax.nn.sigmoid(pre)
        return pre * sigma, (cott[i] * sigma * (1.0 + pre * (1.0 - sigma))).astype(BF)

    across = (((1,), (1,)), ((), ()))
    half = pl.ds(pl.multiple_of(c * 64, 64), 64)
    result, dpre_t = layer(0)
    _, other_t = layer(1)
    gfull = jnp.dot(wn[half, :], dpre_t, preferred_element_type=F32)
    gfull = gfull + jnp.dot(wn2[half, :], other_t, preferred_element_type=F32)
    gfull = (gfull * inverse).astype(BF)
    gx[0, x, y] = gfull[0:32]
    gy[0, y, x] = gfull[32:64]

    near = (0, 7, 1, 6, 2, 5, 3, 4)
    for k in SPREAD:
        push(gx.at[0, x, y], gx.at[0, x, y], sb.at[0], rbx.at[0], dev(x, yp(k), z, c))
        push(gy.at[0, y, x], gy.at[0, y, x], sb.at[1], rby.at[0], dev(xp(k), y, z, c))
    for q in range(NZ - 1, 2, -1):
        to = dev(x, y, zp(NZ - near[q]), c)
        push(gx.at[0, x, y], gx.at[q, x, y], sa.at[0], ra.at[q], to)
        push(gy.at[0, y, x], gy.at[q, y, x], sa.at[1], ra.at[q], to)
    owe(gx.at[pl.ds(0, 5), 0, 0], sa.at[0])
    owe(gy.at[pl.ds(0, 5), 0, 0], sa.at[1])

    dpre = dpre_t.astype(F32).T.astype(BF)
    grad_s = jnp.dot(xt[...], dpre, preferred_element_type=F32)
    grad_n = jnp.dot(mean_tb, dpre, preferred_element_type=F32)
    w0[:, 0:8, :] = grad_s.reshape(16, 8, B)
    w0[:, 8:16, :] = grad_n.reshape(16, 8, B)
    here = x * NY + y
    plane = [(i, j) for i in (2, 1, 3, 0) for j in (2, 1, 3, 0) if (i, j) != (0, 0)]
    for i, j in plane:
        push(w0.at[xp(i) * NY + yp(j)], rw1.at[here], sw.at[0], rw.at[0], dev(xp(i), yp(j), z, c))
    owe(rw1.at[pl.ds(0, 15)], sw.at[0])
    direct = lax.dot_general(dpre, ws[...], across, preferred_element_type=F32)
    out_o[...] = result.T.astype(BF)
    emit = [pltpu.make_async_copy(out_o, out_h, out_sem.at[0])]
    emit[0].start()

    def across_second(q):
        take(gx.at[q, x, pl.ds(0, 2)], ra.at[q])
        for k in SPREAD:
            push(gx.at[q, x, y], gx.at[q, x, y], sb.at[0], rbx.at[q], dev(x, yp(k), z, c))
            push(gy.at[q, y, x], gy.at[q, y, x], sb.at[1], rby.at[q], dev(xp(k), y, z, c))

    def across_third(q):
        take(gx.at[q, x, pl.ds(0, 3)], rbx.at[q])
        for k in SPREAD:
            push(gx.at[q, x], gx.at[q, x], sc.at[0], rcx.at[q], dev(xp(k), y, z, c))
        take(gy.at[q, y, pl.ds(0, 3)], rby.at[q])
        for k in SPREAD:
            push(gy.at[q, y], gy.at[q, y], sc.at[1], rcy.at[q], dev(x, yp(k), z, c))

    def plane_to_next():
        take(gx.at[0, pl.ds(0, 3)], rcx.at[0])
        take(gy.at[0, pl.ds(0, 3)], rcy.at[0])
        for q in (1, 2):
            to = dev(x, y, zp(NZ - near[q]), c)
            push(gx.at[0], gx.at[q], sc.at[2], rbx.at[q], to)
            push(gy.at[0], gy.at[q], sc.at[3], rby.at[q], to)

    def last_phase(q, acc):
        if q in (1, 2):
            take(gx.at[q], rbx.at[q])
            take(gy.at[q], rby.at[q])
        elif q > 2:
            take(gx.at[q, pl.ds(0, 3)], rcx.at[q])
            take(gy.at[q, pl.ds(0, 3)], rcy.at[q])
        for py in range(NY):
            right = jnp.concatenate(
                [jnp.concatenate([gx[q, px, py], gy[q, py, px]], axis=0) for px in range(NX)], axis=1
            )
            acc = acc + lax.dot_general(adj[STEPS.index(near[q]), py], right, across, preferred_element_type=F32)
        return acc

    def weights_second():
        rw1[here] = w0[here]
        take(rw1.at[pl.ds(0, 15)], rw.at[0])
        total = rw1[0]
        for k in range(1, 16):
            total = total + rw1[k]
        rw3[z] = total
        for k in range(1, NZ):
            push(rw3.at[z], rw3.at[z], sw.at[1], rw.at[1], dev(x, y, zp(k), c))
        owe(rw3.at[pl.ds(0, 7)], sw.at[1])

    def weights_third():
        take(rw3.at[pl.ds(0, 7)], rw.at[1])
        total = rw3[0]
        for k in range(1, NZ):
            total = total + rw3[k]
        wg[...] = total
        for i, j in plane:
            to = dev(xp(i), yp(j), z, c)
            push(wg.at[pl.ds(0, 8)], gs_h.at[here], sw.at[2], rw.at[2], to)
            push(wg.at[pl.ds(8, 8)], gn_h.at[here], sw.at[2], rw.at[2], to)
        owe(rw1.at[pl.ds(0, 15)], sw.at[2])
        emit.append(pltpu.make_async_copy(wg.at[pl.ds(0, 8)], gs_h.at[here], out_sem.at[1]))
        emit.append(pltpu.make_async_copy(wg.at[pl.ds(8, 8)], gn_h.at[here], out_sem.at[2]))
        emit[1].start()
        emit[2].start()

    acc = jnp.zeros((B, 64), F32)
    weights = {2: weights_second, 3: weights_third}
    for step in PLAN:
        what, q = step[0], int(step[1])
        if what == "s":
            across_second(q)
        elif what == "t":
            across_third(q)
        elif what == "w":
            weights[q]()
        elif what == "r":
            plane_to_next()
        else:
            acc = last_phase(q, acc)
    owe(gx.at[pl.ds(0, 6), 0, pl.ds(0, 3)], sb.at[0])
    owe(gy.at[pl.ds(0, 6), 0, pl.ds(0, 3)], sb.at[1])
    owe(gx.at[pl.ds(0, 6), pl.ds(0, 3)], sc.at[0])
    owe(gy.at[pl.ds(0, 6), pl.ds(0, 3)], sc.at[1])
    owe(gx.at[pl.ds(0, 2)], sc.at[2])
    owe(gy.at[pl.ds(0, 2)], sc.at[3])

    none = jnp.zeros((B, 64), F32)
    placed = jnp.where(c == 0, jnp.concatenate([acc, none], axis=1), jnp.concatenate([none, acc], axis=1))
    gis[...] = placed + direct
    push(gis, gir_h, sg.at[1], rsg.at[3], dev(x, y, z, oc))
    emit.append(pltpu.make_async_copy(gis, gis_h, out_sem.at[3]))
    emit[3].start()
    take(rw1.at[pl.ds(0, 15)], rw.at[2])

    settle()
    take(gis, rsg.at[3])
    take(gis, sg.at[1])
    for copy in emit:
        copy.wait()


def hand_out(out_h, gis_h, gir_h, gs_h, gn_h, out_t, gi_t, gs_t, gn_t, out, gis, gir, gs, gn, gi, sems):
    inward = [
        pltpu.make_async_copy(a, b, sems.at[0, i])
        for i, (a, b) in enumerate(((gis_h, gis), (gir_h, gir), (out_h, out), (gs_h, gs), (gn_h, gn)))
    ]
    outward = [
        pltpu.make_async_copy(a, b, sems.at[1, i])
        for i, (a, b) in enumerate(((gi, gi_t), (out, out_t), (gs, gs_t), (gn, gn_t)))
    ]
    for copy in inward:
        copy.start()
    inward[0].wait()
    inward[1].wait()
    gi[...] = (gis[...] + gir[...]).astype(BF)
    outward[0].start()
    for first, second in zip(inward[2:], outward[1:]):
        first.wait()
        second.start()
    for copy in outward:
        copy.wait()


def on_device(features, w_self, w_neigh, tiles, dest, outside, cotangent):
    hbm = pl.BlockSpec(memory_space=pltpu.HBM)
    dma = pltpu.SemaphoreType.DMA
    V = pltpu.VMEM
    results = pl.pallas_call(
        kernel,
        out_shape=(
            jax.ShapeDtypeStruct((B, B), BF),
            jax.ShapeDtypeStruct((B, B), F32),
            jax.ShapeDtypeStruct((B, B), F32),
            jax.ShapeDtypeStruct((16, 8, B), F32),
            jax.ShapeDtypeStruct((16, 8, B), F32),
        ),
        in_specs=[hbm] * 7,
        out_specs=(hbm,) * 5,
        scratch_shapes=[
            V((B, B), BF), V((B, B), BF), V((B, B), BF), V((1, B), jnp.int32), V((1, B), jnp.int32),
            V((B, B), BF), V((B, B), BF),
            V((B, B), BF), V((B, B), BF), V((B, B), BF),
            V((B + 1, B, B), BF),
            V((NZ, NY, B, NX * B), BF),
            V((B, B), BF),
            V((8, B), jnp.int32),
            pltpu.SMEM((8, B), jnp.int32),
            V((2, B, B), F32),
            V((2, B, B), BF),
            V((2, B, B), F32),
            V((NZ, NX, NY, 32, B), BF),
            V((NZ, NY, NX, 32, B), BF),
            V((NZ, 3, NY, 32, B), BF),
            V((NZ, 3, NX, 32, B), BF),
            V((NZ, NY, 32, B), BF),
            V((NZ, NX, 32, B), BF),
            V((3, NY, 32, B), BF),
            V((3, NX, 32, B), BF),
            V((2, NX, NY, 32, B), BF),
            V((2, NY, NX, 32, B), BF),
            V((2, NX, 4, B), F32),
            V((2, NY, 32, B), BF),
            V((2, NX, 32, B), BF),
            V((NY, 32, B), BF),
            V((NX, 32, B), BF),
            V((16, 32, B), BF),
            V((NZ, NX, 4, B), F32),
            V((NZ, 3, 4, B), F32),
            V((NZ, 4, B), F32),
            V((5, 4, B), F32),
            V((4, B), F32),
            V((3, 4, B), F32),
            V((NZ, NX, NY, 32, B), BF),
            V((NZ, NY, NX, 32, B), BF),
            V((16, 16, B), F32),
            V((16, 16, B), F32),
            V((NZ, 16, B), F32),
            V((16, B), F32),
            V((B, B), F32),
            dma((11,)),
            dma((5,)), dma((3,)), dma((NZ,)), dma((NZ,)),
            dma((2,)), dma((2,)), dma((2, 2)),
            dma(()), dma(()),
            dma((3,)), dma((3,)), dma((NZ,)),
            dma((5,)), dma((4,)),
            dma((2,)), dma((NZ,)),
            dma((2,)), dma((NZ,)), dma((NZ,)),
            dma((4,)), dma((NZ,)), dma((NZ,)),
            dma((3,)), dma((3,)),
            dma((4,)),
            pltpu.SemaphoreType.REGULAR,
        ],
        compiler_params=pltpu.CompilerParams(
            collective_id=0, has_side_effects=True, vmem_limit_bytes=60 * 2**20
        ),
        name="sage",
    )(features, w_self, w_neigh, tiles, dest.reshape(1, B), outside.reshape(1, B), cotangent)
    results = pl.pallas_call(
        hand_out,
        out_shape=tuple(jax.ShapeDtypeStruct(r.shape, t) for r, t in zip((results[0],) + results[2:], (BF, BF, F32, F32))),
        in_specs=[hbm] * 5,
        out_specs=(hbm,) * 4,
        scratch_shapes=[V(r.shape, r.dtype) for r in results] + [V((B, B), BF), dma((2, 5))],
        compiler_params=pltpu.CompilerParams(vmem_limit_bytes=60 * 2**20),
        name="hand_out",
    )(*results)
    output, grad_input, grad_self, grad_neigh = results
    return output, grad_input, grad_self.reshape(B, B), grad_neigh.reshape(B, B)


def solution(mesh):
    placed = (
        P("dom", None),
        P(None, "feat"),
        P(None, "feat"),
        P("dom", None, None),
        P("dom", None),
        P("dom"),
        P("dom", "feat"),
    )
    return jax.shard_map(
        on_device,
        mesh=mesh,
        in_specs=placed,
        out_specs=(P("dom", "feat"), P("dom", None), P(None, "feat"), P(None, "feat")),
        check_vma=False,
    )
```
